32 devices in a mesh: day: 2 (over y), tile: 4 (over z), freq: 2 (over x), sub: 2 (over core).
Axes of the slice: x: 2, y: 2, z: 4, core: 2. Of those that a mesh axis runs over, the one named last changes fastest.
Arguments:
- spectra: float32 [4, 16, 256, 1024], P('day', None, 'freq', ('tile', 'sub')), parts along dimension 0, may hold values from -6 to 6
- pair_list: int32 [6, 2], replicated, may hold values from 0 to 7, as said below
- owner_slots: int32 [4, 2], replicated, may hold values from -1 to 5, as said below
Outputs:
- lagged: float32 [128, 16, 256, 128], P(('sub', 'freq'), ('day', 'tile')), parts along dimension 1
The draws below stay inside these ranges and needn't reach their ends.
There are 2 independent parts, one for each index of `day`. The reference program is written for one: setup_inputs(seed, part) draws one part's arguments, and reference() takes and returns one part's arrays. A program takes and returns all parts, laid end to end along the dimension named above; an argument that names none is the same for every part. Nothing has to cross between parts.
Inputs may be any that keep to these rules, and one draw needn't show every extreme that they name: `pair_list`: each row names a block and then a block 0 to 3 further along; the first row starts at block 0 and the last row starts at the last block. `owner_slots`: every pair number appears exactly once; -1 marks an empty slot; some owner has all 2 slots filled.
All inputs are finite; a program needn't handle non-finite values.
Results may differ from the reference program's by a relative error of at most 0.0003.
Values sent between devices are 32-bit elements; how exact they have to be, the bound alone decides.
No kernel may reach another device: no remote copies, remote signals or barrier semaphores. Data moves between devices by JAX's collectives and lax.ppermute only.
A program may use at most 128 MiB of HBM per device.

```python
import math
import jax
import jax.numpy as jnp
from jax import lax

WINDOWS = 16
FREQS = 256
LAGS = 256
CH_DEV = 128
CAP = 2
BLOCKS = 8
CHANNELS = 1024
PAIRS = 6
SLOTS = 8


def draw_pair_list(key, part):
    first_key, offset_key = jax.random.split(jax.random.fold_in(key, 11))
    starts = jax.random.randint(first_key, (PAIRS,), 0, BLOCKS)
    starts = starts.at[0].set(0).at[PAIRS - 1].set(BLOCKS - 1)
    offsets = jax.random.randint(offset_key, (PAIRS,), 0, 4)
    end_block = jnp.minimum(starts + offsets, BLOCKS - 1)
    return jnp.stack([starts, end_block], axis=1).astype(jnp.int32)


def draw_owner_slots(key, part):
    order = jax.random.permutation(jax.random.fold_in(key, 23), SLOTS)
    filled = jnp.where(order < PAIRS, order, -1)
    return filled.reshape(SLOTS // CAP, CAP).astype(jnp.int32)


def levels(own_key, extent, cuts, low, top_value):
    factor_of = 1.0
    for dim, shards_of in cuts:
        steps = jax.random.uniform(jax.random.fold_in(jax.random.fold_in(own_key, 6), dim), (shards_of,), jnp.float32, low / len(cuts), top_value / len(cuts))
        factor_of = factor_of * jnp.repeat(jnp.exp(steps), extent[dim] // shards_of).reshape((-1,) + (1,) * (len(extent) - 1 - dim))
    return factor_of


def bell_draw(own_key, extent, width, reach, cuts=(), kind=jnp.bfloat16):
    array = jax.random.normal(own_key, extent, jnp.float32) * width
    if len(cuts) > 0:
        array = levels(own_key, extent, cuts, -0.22, 0.18) * array
    return jnp.clip(array, min=-reach, max=reach).astype(kind)


def setup_inputs(seed: int = 0, part: int = 0) -> dict:
    seeds = jax.random.split(jax.random.key(seed), 4)
    part_keys = jax.random.split(jax.random.fold_in(seeds[3], part), 4)
    return {
        "spectra": bell_draw(part_keys[0], (2, WINDOWS, FREQS, CHANNELS), 1.0, 6.0, ((2, 2), (3, 8)), jnp.float32),
        "pair_list": draw_pair_list(jax.random.fold_in(seeds[3], 71), part),
        "owner_slots": draw_owner_slots(jax.random.fold_in(seeds[3], 71), part),
    }


def whiten(spectra):
    amplitude = jnp.sqrt(spectra[0] * spectra[0] + spectra[1] * spectra[1])
    return spectra / jnp.maximum(amplitude, 1.0)

def lag_table(freq_start, freq_count, total_freq, lag_count):
    freq_ids = freq_start + lax.iota(jnp.int32, freq_count)
    lag_ids = lax.iota(jnp.int32, lag_count) - lag_count // 2
    phases = lag_ids[:, None] * freq_ids[None, :] % (2 * total_freq)
    angles = phases.astype(jnp.float32) * (jnp.pi / total_freq)
    norm_scale = 1.0 / math.sqrt(total_freq)
    return jnp.concatenate([jnp.cos(angles), -jnp.sin(angles)], axis=1) * norm_scale

def reference(spectra, pair_list, owner_slots):
    whitened = whiten(spectra)
    blocks = whitened.reshape(2, WINDOWS, FREQS, BLOCKS, CH_DEV)
    lag_weights = lag_table(0, FREQS, FREQS, LAGS)
    slot_ids = owner_slots.reshape(-1)

    def one_slot(slot_id):
        pair_id = jnp.maximum(slot_id, 0)
        first_block = pair_list[pair_id, 0]
        second_block = pair_list[pair_id, 1]
        row_part = lax.dynamic_index_in_dim(blocks, first_block, 3, keepdims=False)
        col_part = lax.dynamic_index_in_dim(blocks, second_block, 3, keepdims=False)
        turned = jnp.stack([row_part[1], -row_part[0]])
        stacked_rows = jnp.stack([row_part, turned])
        cross_spec = jnp.einsum('ekwfr,kwfc->efrc', stacked_rows, col_part, precision=lax.Precision.HIGHEST)
        cross_spec = cross_spec / math.sqrt(WINDOWS)
        lag_values = jnp.einsum('mq,qrc->rmc', lag_weights, cross_spec.reshape(2 * FREQS, CH_DEV, CH_DEV), precision=lax.Precision.HIGHEST)
        return lag_values * (slot_id >= 0).astype(lag_values.dtype)
    stacked = lax.map(one_slot, slot_ids)
    return jnp.transpose(stacked, (1, 0, 2, 3))
```

```python
import functools
import math

import jax
import jax.numpy as jnp
import ml_dtypes
import numpy as np
from jax import lax
from jax.experimental import pallas as pl
from jax.experimental.pallas import tpu as pltpu
from jax.sharding import PartitionSpec as P

FREQS = 256
LAGS = 256
BF16 = jnp.bfloat16
VMEM_LIMIT = 56 * 1024 * 1024


def lag_tables(scale):
    lag_ids = np.arange(LAGS) - LAGS // 2
    phases = (lag_ids[:, None] * np.arange(FREQS)[None, :]) % (2 * FREQS)
    angles = phases * (np.pi / FREQS)
    table = np.concatenate([np.cos(angles), -np.sin(angles)], axis=1) * scale
    head = table.astype(ml_dtypes.bfloat16)
    tail = (table - head.astype(np.float64)).astype(ml_dtypes.bfloat16)
    return np.concatenate([head, tail], axis=0)


def split(x):
    head = x.astype(BF16)
    return head, (x - head.astype(jnp.float32)).astype(BF16)


def whiten_kernel(part_ref, x_ref, o_ref):
    parts, windows, chunk, width = x_ref.shape
    for f in range(chunk):
        re = x_ref[0, :, f, :]
        im = x_ref[1, :, f, :]
        amplitude = jnp.maximum(jnp.sqrt(re * re + im * im), 1.0)
        o_ref[f, :windows, :] = re / amplitude
        o_ref[f, windows:, :] = im / amplitude


def whiten(spectra, part, fq):
    parts, windows, _, width = spectra.shape
    chunk = 16
    steps = fq // chunk
    return pl.pallas_call(
        whiten_kernel,
        grid_spec=pltpu.PrefetchScalarGridSpec(
            num_scalar_prefetch=1,
            grid=(steps,),
            in_specs=[pl.BlockSpec((parts, windows, chunk, width), lambda i, p: (0, 0, p[0] * steps + i, 0))],
            out_specs=pl.BlockSpec((chunk, parts * windows, width), lambda i, p: (i, 0, 0)),
        ),
        out_shape=jax.ShapeDtypeStruct((fq, parts * windows, width), jnp.float32),
        compiler_params=pltpu.CompilerParams(vmem_limit_bytes=VMEM_LIMIT),
        cost_estimate=pl.CostEstimate(flops=fq * 32 * width * 8, bytes_accessed=fq * 32 * width * 8, transcendentals=0),
        name="whiten",
    )(part.reshape(1), spectra)


def corr_kernel(nq, items, rows, slots, meta, *refs):
    srcs = refs[: nq * items]
    table, mask, out = refs[nq * items : nq * items + 3]
    row_buf, col_buf, cross, out_buf, in_sem, out_sem = refs[nq * items + 3 :]
    fq, kw, width = row_buf.shape[2:]
    group = 4
    packs = width // rows
    per_pack = group * packs
    m_rows = group * 2 * rows

    def fetch(slot):
        for which, buf in ((0, row_buf), (1, col_buf)):
            item = meta[1 + nq + 3 * slot + which]
            for q in range(nq):
                for n in range(items):

                    @pl.when(jnp.logical_and(item == n, meta[1 + nq + 3 * slot + 2] > 0))
                    def _():
                        pltpu.make_async_copy(srcs[q * items + n], buf.at[slot, q], in_sem.at[slot, which, q]).start()

    def wait_fetch(slot, q):
        for which, buf in ((0, row_buf), (1, col_buf)):
            pltpu.make_async_copy(srcs[0], buf.at[slot, q], in_sem.at[slot, which, q]).wait()

    def out_copy(slot, pair, buf):
        return pltpu.make_async_copy(out_buf.at[buf], out.at[pl.ds(pair * 2, 2), slot], out_sem.at[buf])

    for slot in range(slots):
        fetch(slot)

    lane = lax.broadcasted_iota(jnp.int32, (width, width), 1)
    for slot in range(slots):
        filled = meta[1 + nq + 3 * slot + 2] > 0

        @pl.when(filled)
        def _():
            for q in range(nq):
                wait_fetch(slot, q)

                @pl.loop(0, fq // per_pack)
                def _(p):
                    packed = jnp.zeros((width, width), jnp.float32)
                    for g in range(packs):
                        part = row_buf[slot, q, pl.ds(p * per_pack + g * group, group)].reshape(group * kw, width)
                        shift = lax.rem(meta[0] + g * rows, width)
                        packed = jnp.where(lane // rows == g, pltpu.roll(part, shift, 1), packed)
                    turned = packed.T
                    swapped = jnp.where(
                        lane % kw < kw // 2, pltpu.roll(turned, width - kw // 2, 1), -pltpu.roll(turned, kw // 2, 1)
                    )
                    for g in range(packs):
                        span = slice(g * rows, (g + 1) * rows)
                        head, tail = split(jnp.concatenate([turned[span], swapped[span]], axis=0))
                        left = jnp.concatenate(
                            [
                                jnp.concatenate([head * mask[n], tail * mask[n]], axis=1)
                                for n in range(group)
                            ],
                            axis=0,
                        )
                        part = col_buf[slot, q, pl.ds(p * per_pack + g * group, group)].reshape(group * kw, width)
                        top = jnp.concatenate(split(part), axis=1)
                        both = jnp.dot(left, jnp.concatenate([top, top], axis=0), preferred_element_type=jnp.float32)
                        first = (meta[1 + q] + p * per_pack + g * group) * (2 * rows)
                        cross[pl.ds(pl.multiple_of(first, m_rows), m_rows)] = both[:, :width] + both[:, width:]

        @pl.loop(0, rows // 2)
        def _(pair):
            buf = lax.rem(pair, 2)

            @pl.when(jnp.logical_or(pair >= 2, slot > 0))
            def _():
                out_copy(slot, pair, buf).wait()

            @pl.when(filled)
            def _():
                halves = [
                    jnp.concatenate(
                        [cross[pl.ds(e * rows + pair * 2 + n, FREQS, stride=2 * rows)] for n in range(2)], axis=1
                    )
                    for e in range(2)
                ]
                head, tail = split(jnp.concatenate(halves, axis=0))
                high = jnp.dot(table[...], head, preferred_element_type=jnp.float32)
                low = jnp.dot(table[:LAGS], tail, preferred_element_type=jnp.float32)
                lagged = high[:LAGS] + high[LAGS:] + low
                for n in range(2):
                    out_buf[buf, n] = lagged[:, n * width : (n + 1) * width]

            @pl.when(jnp.logical_not(filled))
            def _():
                out_buf[buf] = jnp.zeros(out_buf.shape[1:], jnp.float32)

            out_copy(slot, pair, buf).start()

    for buf in range(2):
        out_copy(0, 0, buf).wait()


def correlate(meta, srcs, rows, slots, windows):
    nq, items = len(srcs), len(srcs[0])
    fq, kw, width = srcs[0][0].shape
    table = jnp.asarray(lag_tables(1.0 / math.sqrt(windows * FREQS)))
    mask_np = np.broadcast_to((np.arange(width)[None, None, :] // kw) == np.arange(4)[:, None, None], (4, 2 * rows, width))
    mask = jnp.asarray(mask_np.astype(ml_dtypes.bfloat16))
    any_spec = pl.BlockSpec(memory_space=pl.ANY)
    vmem_spec = pl.BlockSpec(memory_space=pltpu.VMEM)
    return pl.pallas_call(
        functools.partial(corr_kernel, nq, items, rows, slots),
        in_specs=[pl.BlockSpec(memory_space=pltpu.SMEM)] + [any_spec] * (nq * items) + [vmem_spec] * 2,
        out_specs=any_spec,
        out_shape=jax.ShapeDtypeStruct((rows, slots, LAGS, width), jnp.float32),
        scratch_shapes=[
            pltpu.VMEM((slots, nq, fq, kw, width), jnp.float32),
            pltpu.VMEM((slots, nq, fq, kw, width), jnp.float32),
            pltpu.VMEM((FREQS * 2 * rows, width), jnp.float32),
            pltpu.VMEM((2, 2, LAGS, width), jnp.float32),
            pltpu.SemaphoreType.DMA((slots, 2, nq)),
            pltpu.SemaphoreType.DMA((2,)),
        ],
        compiler_params=pltpu.CompilerParams(vmem_limit_bytes=VMEM_LIMIT),
        name="correlate",
    )(meta, *[a for share in srcs for a in share], table, mask)


def body(spectra, pair_list, owner_slots):
    tiles = lax.axis_size("tile")
    freq_parts = lax.axis_size("freq")
    subs = lax.axis_size("sub")
    _, windows, band, width = spectra.shape
    slots = owner_slots.shape[1]
    nq = freq_parts * subs
    fq = band // subs
    rows = width // nq
    me_tile, me_freq, me_sub = lax.axis_index("tile"), lax.axis_index("freq"), lax.axis_index("sub")
    swap = [(0, 1), (1, 0)]
    other = whiten(spectra, 1 - me_sub, fq)
    passed = lax.ppermute(other, "sub", swap)
    mine = whiten(spectra, me_sub, fq)
    my_pairs = lax.dynamic_index_in_dim(owner_slots, me_tile, 0, keepdims=False)
    filled = (my_pairs >= 0).astype(jnp.int32)
    wanted = jnp.take(pair_list, jnp.maximum(my_pairs, 0), axis=0)
    shift = (width - (me_sub * freq_parts + me_freq) * rows) % width

    held = lax.all_gather(jnp.stack([mine, passed]), "tile")
    items = []
    for slot in range(slots):
        for which in range(2):
            block = wanted[slot, which]
            chosen = held[block // 2, (block % 2) ^ me_sub]
            items.append(lax.all_gather(chosen, ("freq", "sub")))
    srcs = [[item[q] for item in items] for q in range(nq)]
    first = jnp.arange(nq, dtype=jnp.int32) * fq
    meta = jnp.concatenate(
        [shift.reshape(1), first]
        + [jnp.stack([jnp.int32(2 * k), jnp.int32(2 * k + 1), filled[k]]) for k in range(slots)]
    ).astype(jnp.int32)
    return correlate(meta, srcs, rows, slots, windows)


def solution(mesh):
    in_specs = (P("day", None, "freq", ("tile", "sub")), P(), P())
    out_specs = P(("sub", "freq"), ("day", "tile"), None, None)
    return jax.shard_map(body, mesh=mesh, in_specs=in_specs, out_specs=out_specs, check_vma=False)
```

```python
import functools
import math

import jax
import jax.numpy as jnp
import ml_dtypes
import numpy as np
from jax import lax
from jax.experimental import pallas as pl
from jax.experimental.pallas import tpu as pltpu
from jax.sharding import PartitionSpec as P

FREQS = 256
LAGS = 256
BF16 = jnp.bfloat16
VMEM_LIMIT = 56 * 1024 * 1024


def lag_tables(scale):
    lag_ids = np.arange(LAGS) - LAGS // 2
    phases = (lag_ids[:, None] * np.arange(FREQS)[None, :]) % (2 * FREQS)
    angles = phases * (np.pi / FREQS)
    table = np.concatenate([np.cos(angles), -np.sin(angles)], axis=1) * scale
    head = table.astype(ml_dtypes.bfloat16)
    tail = (table - head.astype(np.float64)).astype(ml_dtypes.bfloat16)
    return np.concatenate([head, tail], axis=0)


def split(x):
    head = x.astype(BF16)
    return head, (x - head.astype(jnp.float32)).astype(BF16)


def whiten_kernel(part_ref, x_ref, o_ref):
    parts, windows, chunk, width = x_ref.shape
    for f in range(chunk):
        re = x_ref[0, :, f, :]
        im = x_ref[1, :, f, :]
        amplitude = jnp.maximum(jnp.sqrt(re * re + im * im), 1.0)
        o_ref[f, :windows, :] = re / amplitude
        o_ref[f, windows:, :] = im / amplitude


def whiten(spectra, part, fq):
    parts, windows, _, width = spectra.shape
    chunk = 16
    steps = fq // chunk
    return pl.pallas_call(
        whiten_kernel,
        grid_spec=pltpu.PrefetchScalarGridSpec(
            num_scalar_prefetch=1,
            grid=(steps,),
            in_specs=[pl.BlockSpec((parts, windows, chunk, width), lambda i, p: (0, 0, p[0] * steps + i, 0))],
            out_specs=pl.BlockSpec((chunk, parts * windows, width), lambda i, p: (i, 0, 0)),
        ),
        out_shape=jax.ShapeDtypeStruct((fq, parts * windows, width), jnp.float32),
        compiler_params=pltpu.CompilerParams(vmem_limit_bytes=VMEM_LIMIT),
        cost_estimate=pl.CostEstimate(flops=fq * 32 * width * 8, bytes_accessed=fq * 32 * width * 8, transcendentals=0),
        name="whiten",
    )(part.reshape(1), spectra)


def corr_kernel(base, nq, items, rows, slots, meta, *refs):
    srcs = refs[: nq * items]
    table, mask, out = refs[nq * items : nq * items + 3]
    row_buf, col_buf, cross, out_buf, in_sem, out_sem = refs[nq * items + 3 :]
    fq, kw, width = row_buf.shape[2:]
    group = 4
    packs = width // rows
    per_pack = group * packs
    m_rows = group * 2 * rows

    def fetch(slot):
        for which, buf in ((0, row_buf), (1, col_buf)):
            item = meta[base + 1 + nq + 3 * slot + which]
            for n in range(items):

                @pl.when(jnp.logical_and(item == n, meta[base + 1 + nq + 3 * slot + 2] > 0))
                def _():
                    for q in range(nq):
                        pltpu.make_async_copy(srcs[q * items + n], buf.at[slot, q], in_sem.at[slot, which, q]).start()

    def wait_fetch(slot, q):
        for which, buf in ((0, row_buf), (1, col_buf)):
            pltpu.make_async_copy(srcs[0], buf.at[slot, q], in_sem.at[slot, which, q]).wait()

    def out_copy(slot, pair, buf):
        return pltpu.make_async_copy(out_buf.at[buf], out.at[pl.ds(pair * 2, 2), slot], out_sem.at[buf])

    for slot in range(slots):
        fetch(slot)

    lane = lax.broadcasted_iota(jnp.int32, (width, width), 1)
    for slot in range(slots):
        filled = meta[base + 1 + nq + 3 * slot + 2] > 0

        @pl.when(filled)
        def _():
            for q in range(nq):
                wait_fetch(slot, q)

                @pl.loop(0, fq // per_pack)
                def _(p):
                    packed = jnp.zeros((width, width), jnp.float32)
                    for g in range(packs):
                        part = row_buf[slot, q, pl.ds(p * per_pack + g * group, group)].reshape(group * kw, width)
                        shift = lax.rem(meta[base] + g * rows, width)
                        packed = jnp.where(lane // rows == g, pltpu.roll(part, shift, 1), packed)
                    turned = packed.T
                    swapped = jnp.where(
                        lane % kw < kw // 2, pltpu.roll(turned, width - kw // 2, 1), -pltpu.roll(turned, kw // 2, 1)
                    )
                    for g in range(packs):
                        span = slice(g * rows, (g + 1) * rows)
                        head, tail = split(jnp.concatenate([turned[span], swapped[span]], axis=0))
                        left = jnp.concatenate(
                            [
                                jnp.concatenate([head * mask[n], tail * mask[n]], axis=1)
                                for n in range(group)
                            ],
                            axis=0,
                        )
                        part = col_buf[slot, q, pl.ds(p * per_pack + g * group, group)].reshape(group * kw, width)
                        top = jnp.concatenate(split(part), axis=1)
                        both = jnp.dot(left, jnp.concatenate([top, top], axis=0), preferred_element_type=jnp.float32)
                        first = (meta[base + 1 + q] + p * per_pack + g * group) * (2 * rows)
                        cross[pl.ds(pl.multiple_of(first, m_rows), m_rows)] = both[:, :width] + both[:, width:]

        @pl.loop(0, rows // 2)
        def _(pair):
            buf = lax.rem(pair, 2)

            @pl.when(jnp.logical_or(pair >= 2, slot > 0))
            def _():
                out_copy(slot, pair, buf).wait()

            @pl.when(filled)
            def _():
                halves = [
                    jnp.concatenate(
                        [cross[pl.ds(e * rows + pair * 2 + n, FREQS, stride=2 * rows)] for n in range(2)], axis=1
                    )
                    for e in range(2)
                ]
                head, tail = split(jnp.concatenate(halves, axis=0))
                high = jnp.dot(table[...], head, preferred_element_type=jnp.float32)
                low = jnp.dot(table[:LAGS], tail, preferred_element_type=jnp.float32)
                lagged = high[:LAGS] + high[LAGS:] + low
                for n in range(2):
                    out_buf[buf, n] = lagged[:, n * width : (n + 1) * width]

            @pl.when(jnp.logical_not(filled))
            def _():
                out_buf[buf] = jnp.zeros(out_buf.shape[1:], jnp.float32)

            out_copy(slot, pair, buf).start()

    for buf in range(2):
        out_copy(0, 0, buf).wait()


def correlate(meta, base, srcs, rows, slots, windows):
    nq, items = len(srcs), len(srcs[0])
    fq, kw, width = srcs[0][0].shape
    table = jnp.asarray(lag_tables(1.0 / math.sqrt(windows * FREQS)))
    mask_np = np.broadcast_to((np.arange(width)[None, None, :] // kw) == np.arange(4)[:, None, None], (4, 2 * rows, width))
    mask = jnp.asarray(mask_np.astype(ml_dtypes.bfloat16))
    any_spec = pl.BlockSpec(memory_space=pl.ANY)
    vmem_spec = pl.BlockSpec(memory_space=pltpu.VMEM)
    return pl.pallas_call(
        functools.partial(corr_kernel, base, nq, items, rows, slots),
        in_specs=[pl.BlockSpec(memory_space=pltpu.SMEM)] + [any_spec] * (nq * items) + [vmem_spec] * 2,
        out_specs=any_spec,
        out_shape=jax.ShapeDtypeStruct((rows, slots, LAGS, width), jnp.float32),
        scratch_shapes=[
            pltpu.VMEM((slots, nq, fq, kw, width), jnp.float32),
            pltpu.VMEM((slots, nq, fq, kw, width), jnp.float32),
            pltpu.VMEM((FREQS * 2 * rows, width), jnp.float32),
            pltpu.VMEM((2, 2, LAGS, width), jnp.float32),
            pltpu.SemaphoreType.DMA((slots, 2, nq)),
            pltpu.SemaphoreType.DMA((2,)),
        ],
        compiler_params=pltpu.CompilerParams(vmem_limit_bytes=VMEM_LIMIT),
        name="correlate",
    )(meta, *[a for share in srcs for a in share], table, mask)


def plan_kernel(tiles, subs, slots, rounds, chunks, fq, rows, width, pair_ref, owner_ref, plan_ref):
    me, me_freq, me_sub = lax.axis_index("tile"), lax.axis_index("freq"), lax.axis_index("sub")
    freqs = lax.axis_size("freq")
    zero = jnp.int32(0)

    def bit(block):
        return jnp.left_shift(jnp.int32(1), block)

    def own(tile):
        return ((1 << subs) - 1) << (subs * tile)

    def up_to(tile):
        return (1 << (subs * (tile + 1))) - 1

    def pick(index, values):
        chosen = zero
        for key, value in values.items():
            chosen = jnp.where(index == key, value, chosen)
        return chosen

    def lowest(bits):
        return jnp.bitwise_and(bits, -bits)

    every = [[zero] * slots for _ in range(tiles)]
    rows_bit, cols_bit, filled = {}, {}, {}
    for k in range(slots):
        rows_bit[k], cols_bit[k], filled[k] = zero, zero, zero
        for t in range(tiles):
            pair = owner_ref[t, k]
            there = pair >= 0
            first = jnp.where(there, bit(pair_ref[jnp.maximum(pair, 0), 0]), 0)
            second = jnp.where(there, bit(pair_ref[jnp.maximum(pair, 0), 1]), 0)
            every[t][k] = first | second
            mine = me == t
            rows_bit[k] = jnp.where(mine, first, rows_bit[k])
            cols_bit[k] = jnp.where(mine, second, cols_bit[k])
            filled[k] = jnp.where(mine, there.astype(jnp.int32), filled[k])
    need = [functools.reduce(jnp.bitwise_or, every[t]) for t in range(tiles)]
    left_to_do = {}
    for t in range(tiles - 1):
        left_to_do[(1, t)] = functools.reduce(jnp.bitwise_or, need[t + 1 :]) & up_to(t)
        left_to_do[(-1, t + 1)] = functools.reduce(jnp.bitwise_or, need[: t + 1]) & ~up_to(t)
    todo = list(need)
    have = [jnp.int32(own(t)) for t in range(tiles)]
    places = [(bit(subs * me + me_sub), 0), (bit(subs * me + 1 - me_sub), 1)]

    def place(block_bit):
        where = jnp.int32(-1)
        for held_bit, index in places:
            where = jnp.where(jnp.logical_and(block_bit == held_bit, block_bit != 0), index, where)
        return where

    needed_rounds = jnp.int32(1)
    my_order = []
    for r in range(rounds):
        sel, over_freq = {}, {}
        for (step, t), want in left_to_do.items():
            cand = have[t] & want
            chosen = zero
            for u in range(tiles - 1, t, -1) if step > 0 else range(0, t):
                chosen = jnp.where(chosen == 0, lowest(cand & need[u]), chosen)
            sel[(step, t)] = chosen
        for t in range(tiles):
            ready = have[t] & todo[t]
            early = ready & every[t][0]
            over_freq[t] = jnp.where(early != 0, lowest(early), lowest(ready))
        for key in sel:
            left_to_do[key] = left_to_do[key] & ~sel[key]
        for t in range(tiles):
            todo[t] = todo[t] & ~over_freq[t]
            for step in (1, -1):
                if (step, t - step) in sel:
                    have[t] = have[t] | sel[(step, t - step)]
        plan_ref[3 * r] = place(pick(me, {t: sel[(1, t)] for t in range(tiles - 1)}))
        plan_ref[3 * r + 1] = place(pick(me, {t: sel[(-1, t)] for t in range(1, tiles)}))
        mine = pick(me, over_freq)
        plan_ref[3 * r + 2] = place(mine)
        my_order.append(mine)
        places.append((pick(me, {t + 1: sel[(1, t)] for t in range(tiles - 1)}), 2 + 2 * r))
        places.append((pick(me, {t - 1: sel[(-1, t)] for t in range(1, tiles)}), 3 + 2 * r))
        rest = functools.reduce(jnp.bitwise_or, todo)
        needed_rounds = needed_rounds + (rest != 0).astype(jnp.int32)
    plan_ref[3 * rounds] = needed_rounds
    base = 3 * rounds + 1
    plan_ref[base] = lax.rem(width - (me_sub * freqs + me_freq) * rows, width)
    n = 0
    for f, s in ((0, 0), (1, 0), (0, 1), (1, 1)):
        share = (me_freq ^ f) * subs + (me_sub ^ s)
        for c in range(chunks):
            plan_ref[base + 1 + n] = share * fq + c * (fq // chunks)
            n += 1
    for k in range(slots):
        for which, wanted in ((0, rows_bit[k]), (1, cols_bit[k])):
            at = zero
            for r in range(rounds):
                at = jnp.where(my_order[r] == wanted, r, at)
            plan_ref[base + 1 + n + 3 * k + which] = at
        plan_ref[base + 1 + n + 3 * k + 2] = filled[k]


def make_plan(pair_list, owner_slots, rounds, chunks, fq, rows, width):
    tiles, slots = owner_slots.shape
    smem = pl.BlockSpec(memory_space=pltpu.SMEM)
    return pl.pallas_call(
        functools.partial(plan_kernel, tiles, lax.axis_size("sub"), slots, rounds, chunks, fq, rows, width),
        in_specs=[smem, smem],
        out_specs=smem,
        out_shape=jax.ShapeDtypeStruct((3 * rounds + 2 + 4 * chunks + 3 * slots,), jnp.int32),
        name="make_plan",
    )(pair_list, owner_slots)


def choose_kernel(which, chunk, spans, unread, plan, *refs):
    count = len(which)
    held, outs = refs[: len(spans)], refs[len(spans) + unread : len(spans) + unread + count]
    stage, in_sems, out_sems = refs[len(spans) + unread + count :]
    depth = stage.shape[1]

    def load(i, n):
        src = held[n].at[pl.ds(chunk * depth, depth)] if spans[n] else held[n]
        return pltpu.make_async_copy(src, stage.at[i], in_sems.at[i])

    def store(i):
        return pltpu.make_async_copy(stage.at[i], outs[i], out_sems.at[i])

    for i, entry in enumerate(which):
        for n in range(len(spans)):

            @pl.when(plan[entry] == n)
            def _():
                load(i, n).start()

    for i, entry in enumerate(which):

        @pl.when(plan[entry] >= 0)
        def _():
            load(i, 0).wait()
            store(i).start()

    for i, entry in enumerate(which):

        @pl.when(plan[entry] >= 0)
        def _():
            store(i).wait()


def choose(plan, which, held, after, chunk, depth):
    spans = [a.shape[0] != depth for a in held]
    any_spec = pl.BlockSpec(memory_space=pl.ANY)
    out = jax.ShapeDtypeStruct((depth,) + held[0].shape[1:], jnp.float32)
    return pl.pallas_call(
        functools.partial(choose_kernel, which, chunk, spans, len(after)),
        in_specs=[pl.BlockSpec(memory_space=pltpu.SMEM)] + [any_spec] * (len(held) + len(after)),
        out_specs=[any_spec] * len(which),
        out_shape=[out] * len(which),
        scratch_shapes=[
            pltpu.VMEM((len(which),) + out.shape, jnp.float32),
            pltpu.SemaphoreType.DMA((len(which),)),
            pltpu.SemaphoreType.DMA((len(which),)),
        ],
        compiler_params=pltpu.CompilerParams(vmem_limit_bytes=VMEM_LIMIT),
        cost_estimate=pl.CostEstimate(flops=0, bytes_accessed=len(which) * 2 * depth * 32 * 512, transcendentals=0),
        name="choose",
    )(plan, *held, *after)


ROUNDS = 6
CHUNKS = 2


def gather_all(slots, rows, windows, mine, passed, pair_list, owner_slots):
    freq_parts, subs = lax.axis_size("freq"), lax.axis_size("sub")
    me_tile, me_freq, me_sub = lax.axis_index("tile"), lax.axis_index("freq"), lax.axis_index("sub")
    fq, _, width = mine.shape
    nq = freq_parts * subs
    my_pairs = lax.dynamic_index_in_dim(owner_slots, me_tile, 0, keepdims=False)
    filled = (my_pairs >= 0).astype(jnp.int32)
    wanted = jnp.take(pair_list, jnp.maximum(my_pairs, 0), axis=0)
    shift = (width - (me_sub * freq_parts + me_freq) * rows) % width
    held = lax.all_gather(jnp.stack([mine, passed]), "tile")
    items = []
    for slot in range(slots):
        for which in range(2):
            block = wanted[slot, which]
            chosen = held[block // 2, (block % 2) ^ me_sub]
            items.append(lax.all_gather(chosen, ("freq", "sub")))
    srcs = [[item[q] for item in items] for q in range(nq)]
    first = jnp.arange(nq, dtype=jnp.int32) * fq
    meta = jnp.concatenate(
        [shift.reshape(1), first]
        + [jnp.stack([jnp.int32(2 * k), jnp.int32(2 * k + 1), filled[k]]) for k in range(slots)]
    ).astype(jnp.int32)
    return correlate(meta, 0, srcs, rows, slots, windows)


def in_rounds(count, slots, rows, windows, mine, passed, plan):
    tiles = lax.axis_size("tile")
    right = [(t, t + 1) for t in range(tiles - 1)]
    left = [(t + 1, t) for t in range(tiles - 1)]
    swap = [(0, 1), (1, 0)]
    depth = mine.shape[0] // CHUNKS
    held = [[mine, passed] for _ in range(CHUNKS)]
    srcs = [[] for _ in range(4 * CHUNKS)]
    for r in range(count):
        for c in range(CHUNKS):
            after = [srcs[n * CHUNKS + c][r - age] for n, age in ((1, 1), (2, 1), (3, 2)) if r >= age]
            if r < count - 1:
                to_right, to_left, to_freq = choose(plan, (3 * r, 3 * r + 1, 3 * r + 2), held[c], after, c, depth)
                held[c] = held[c] + [lax.ppermute(to_right, "tile", right), lax.ppermute(to_left, "tile", left)]
            else:
                (to_freq,) = choose(plan, (3 * r + 2,), held[c], after, c, depth)
            crossed = lax.ppermute(to_freq, "freq", swap)
            srcs[c].append(to_freq)
            srcs[CHUNKS + c].append(crossed)
            srcs[2 * CHUNKS + c].append(lax.ppermute(to_freq, "sub", swap))
            srcs[3 * CHUNKS + c].append(lax.ppermute(crossed, "sub", swap))
    return correlate(plan, 3 * ROUNDS + 1, srcs, rows, slots, windows)


def body(spectra, pair_list, owner_slots):
    tiles, freq_parts, subs = lax.axis_size("tile"), lax.axis_size("freq"), lax.axis_size("sub")
    _, windows, band, width = spectra.shape
    slots = owner_slots.shape[1]
    fq = band // subs
    rows = width // (freq_parts * subs)
    me_sub = lax.axis_index("sub")
    other = whiten(spectra, 1 - me_sub, fq)
    passed = lax.ppermute(other, "sub", [(0, 1), (1, 0)])
    mine = whiten(spectra, me_sub, fq)
    whole = functools.partial(gather_all, slots, rows, windows)
    if freq_parts != 2 or tiles > 4:
        return whole(mine, passed, pair_list, owner_slots)
    plan = make_plan(pair_list, owner_slots, ROUNDS, CHUNKS, fq, rows, width)
    branches = [
        functools.partial(lambda n, a, b, p, pairs, owners: in_rounds(n, slots, rows, windows, a, b, p), n)
        for n in range(2, ROUNDS + 1)
    ]
    branches.append(lambda a, b, p, pairs, owners: whole(a, b, pairs, owners))
    return lax.switch(
        jnp.maximum(plan[3 * ROUNDS], 2) - 2, branches, mine, passed, plan, pair_list, owner_slots
    )


def solution(mesh):
    in_specs = (P("day", None, "freq", ("tile", "sub")), P(), P())
    out_specs = P(("sub", "freq"), ("day", "tile"), None, None)
    return jax.shard_map(body, mesh=mesh, in_specs=in_specs, out_specs=out_specs, check_vma=False)
```

```python
import functools
import math

import jax
import jax.numpy as jnp
import ml_dtypes
import numpy as np
from jax import lax
from jax.experimental import pallas as pl
from jax.experimental.pallas import tpu as pltpu
from jax.sharding import PartitionSpec as P

FREQS = 256
LAGS = 256
BF16 = jnp.bfloat16
VMEM_LIMIT = 56 * 1024 * 1024
UNROLL = 4
OUT_ROWS = 8


def lag_tables(scale):
    lag_ids = np.arange(LAGS) - LAGS // 2
    phases = (lag_ids[:, None] * np.arange(FREQS)[None, :]) % (2 * FREQS)
    angles = phases * (np.pi / FREQS)
    table = np.concatenate([np.cos(angles), -np.sin(angles)], axis=1) * scale
    head = table.astype(ml_dtypes.bfloat16)
    tail = (table - head.astype(np.float64)).astype(ml_dtypes.bfloat16)
    return np.concatenate([head, tail], axis=0)


def split(x):
    head = x.astype(BF16)
    return head, (x - head.astype(jnp.float32)).astype(BF16)


def whiten_kernel(part_ref, x_ref, o_ref):
    parts, windows, chunk, width = x_ref.shape
    for f in range(chunk):
        re = x_ref[0, :, f, :]
        im = x_ref[1, :, f, :]
        amplitude = jnp.maximum(jnp.sqrt(re * re + im * im), 1.0)
        o_ref[f, :windows, :] = re / amplitude
        o_ref[f, windows:, :] = im / amplitude


def whiten(spectra, part, fq):
    parts, windows, _, width = spectra.shape
    chunk = 16
    steps = fq // chunk
    return pl.pallas_call(
        whiten_kernel,
        grid_spec=pltpu.PrefetchScalarGridSpec(
            num_scalar_prefetch=1,
            grid=(steps,),
            in_specs=[pl.BlockSpec((parts, windows, chunk, width), lambda i, p: (0, 0, p[0] * steps + i, 0))],
            out_specs=pl.BlockSpec((chunk, parts * windows, width), lambda i, p: (i, 0, 0)),
        ),
        out_shape=jax.ShapeDtypeStruct((fq, parts * windows, width), jnp.float32),
        compiler_params=pltpu.CompilerParams(vmem_limit_bytes=VMEM_LIMIT),
        cost_estimate=pl.CostEstimate(flops=fq * 32 * width * 8, bytes_accessed=fq * 32 * width * 8, transcendentals=0),
        name="whiten",
    )(part.reshape(1), spectra)


def corr_kernel(base, nq, items, rows, slots, early, late, unread, meta, *refs):
    srcs = refs[: nq * items]
    table, mask = refs[nq * items : nq * items + 2]
    out, row_buf, col_buf, cross, out_buf, in_sem, out_sem = refs[nq * items + 2 + unread + (late is True) :]
    fq, kw, width = row_buf.shape[2:]
    group = 4
    packs = width // rows
    per_pack = group * packs
    m_rows = group * 2 * rows
    out_rows = out_buf.shape[1]

    def entry(slot, n):
        return meta[base + 1 + nq + 3 * slot + n]

    def in_turn(slot):
        filled = entry(slot, 2) > 0
        if late is None:
            return filled
        ready = jnp.maximum(entry(slot, 0), entry(slot, 1)) < early
        return jnp.logical_and(filled, jnp.logical_not(ready) if late else ready)

    def fetch(slot):
        for which, buf in ((0, row_buf), (1, col_buf)):
            item = entry(slot, which)
            for n in range(items):

                @pl.when(jnp.logical_and(item == n, in_turn(slot)))
                def _():
                    for q in range(nq):
                        pltpu.make_async_copy(srcs[q * items + n], buf.at[slot, q], in_sem.at[slot, which, q]).start()

    def wait_fetch(slot, q):
        for which, buf in ((0, row_buf), (1, col_buf)):
            pltpu.make_async_copy(srcs[0], buf.at[slot, q], in_sem.at[slot, which, q]).wait()

    def out_copy(slot, step, buf):
        return pltpu.make_async_copy(out_buf.at[buf], out.at[pl.ds(step * out_rows, out_rows), slot], out_sem.at[buf])

    @pl.loop(0, slots)
    def _(slot):
        fetch(slot)

    per_share = fq // per_pack
    together = max(1, UNROLL // per_share)
    lane = lax.broadcasted_iota(jnp.int32, (width, width), 1)

    def cross_pack(slot, q, p):
        packed = jnp.zeros((width, width), jnp.float32)
        for g in range(packs):
            part = row_buf[slot, q, pl.ds(p * per_pack + g * group, group)].reshape(group * kw, width)
            shift = lax.rem(meta[base] + g * rows, width)
            packed = jnp.where(lane // rows == g, pltpu.roll(part, shift, 1), packed)
        turned = packed.T
        swapped = jnp.where(
            lane % kw < kw // 2, pltpu.roll(turned, width - kw // 2, 1), -pltpu.roll(turned, kw // 2, 1)
        )
        for g in range(packs):
            span = slice(g * rows, (g + 1) * rows)
            head, tail = split(jnp.concatenate([turned[span], swapped[span]], axis=0))
            left = jnp.concatenate(
                [jnp.concatenate([head * mask[n], tail * mask[n]], axis=1) for n in range(group)], axis=0
            )
            part = col_buf[slot, q, pl.ds(p * per_pack + g * group, group)].reshape(group * kw, width)
            top = jnp.concatenate(split(part), axis=1)
            both = jnp.dot(left, jnp.concatenate([top, top], axis=0), preferred_element_type=jnp.float32)
            first = (meta[base + 1 + q] + p * per_pack + g * group) * (2 * rows)
            cross[pl.ds(pl.multiple_of(first, m_rows), m_rows)] = both[:, :width] + both[:, width:]

    def lag_step(slot, step, buf):
        for pair in range(out_rows // 2):
            halves = [
                jnp.concatenate(
                    [
                        cross[pl.ds(e * rows + step * out_rows + pair * 2 + n, FREQS, stride=2 * rows)]
                        for n in range(2)
                    ],
                    axis=1,
                )
                for e in range(2)
            ]
            head, tail = split(jnp.concatenate(halves, axis=0))
            high = jnp.dot(table[...], head, preferred_element_type=jnp.float32)
            low = jnp.dot(table[:LAGS], tail, preferred_element_type=jnp.float32)
            lagged = high[:LAGS] + high[LAGS:] + low
            for n in range(2):
                out_buf[buf, pair * 2 + n] = lagged[:, n * width : (n + 1) * width]

    steps = rows // out_rows
    @pl.loop(0, slots)
    def _(slot):
        @pl.when(in_turn(slot))
        def _():
            @pl.loop(0, nq // together)
            def _(i):
                for n in range(together):
                    wait_fetch(slot, i * together + n)
                for n in range(together):
                    for p in range(per_share):
                        cross_pack(slot, i * together + n, p)

            @pl.loop(0, steps)
            def _(step):
                buf = lax.rem(step, 2)

                @pl.when(step >= 2)
                def _():
                    out_copy(slot, step, buf).wait()

                lag_step(slot, step, buf)
                out_copy(slot, step, buf).start()

            for buf in range(2):
                out_copy(slot, 0, buf).wait()

        if not late:

            @pl.when(entry(slot, 2) == 0)
            def _():
                out_buf[0] = jnp.zeros(out_buf.shape[1:], jnp.float32)
                for step in range(steps):
                    out_copy(slot, step, 0).start()
                for step in range(steps):
                    out_copy(slot, step, 0).wait()


def correlate(meta, base, srcs, rows, slots, windows, early=0, late=None, after=(), into=None):
    nq, items = len(srcs), len(srcs[0])
    fq, kw, width = srcs[0][0].shape
    table = jnp.asarray(lag_tables(1.0 / math.sqrt(windows * FREQS)))
    mask_np = np.broadcast_to((np.arange(width)[None, None, :] // kw) == np.arange(4)[:, None, None], (4, 2 * rows, width))
    mask = jnp.asarray(mask_np.astype(ml_dtypes.bfloat16))
    any_spec = pl.BlockSpec(memory_space=pl.ANY)
    vmem_spec = pl.BlockSpec(memory_space=pltpu.VMEM)
    operands = [meta, *[a for share in srcs for a in share], table, mask, *after]
    in_specs = [pl.BlockSpec(memory_space=pltpu.SMEM)] + [any_spec] * (nq * items)
    in_specs += [vmem_spec] * 2 + [any_spec] * len(after)
    aliases = {}
    if into is not None:
        aliases = {len(operands): 0}
        operands.append(into)
        in_specs.append(any_spec)
    return pl.pallas_call(
        functools.partial(corr_kernel, base, nq, items, rows, slots, early, late, len(after)),
        in_specs=in_specs,
        out_specs=any_spec,
        out_shape=jax.ShapeDtypeStruct((rows, slots, LAGS, width), jnp.float32),
        scratch_shapes=[
            pltpu.VMEM((slots, nq, fq, kw, width), jnp.float32),
            pltpu.VMEM((slots, nq, fq, kw, width), jnp.float32),
            pltpu.VMEM((FREQS * 2 * rows, width), jnp.float32),
            pltpu.VMEM((2, OUT_ROWS, LAGS, width), jnp.float32),
            pltpu.SemaphoreType.DMA((slots, 2, nq)),
            pltpu.SemaphoreType.DMA((2,)),
        ],
        input_output_aliases=aliases,
        compiler_params=pltpu.CompilerParams(vmem_limit_bytes=VMEM_LIMIT),
        cost_estimate=pl.CostEstimate(
            flops=2 * slots * rows * LAGS * 2 * FREQS * width * 6, bytes_accessed=24 * 1024 * 1024, transcendentals=0
        ),
        name="correlate",
    )(*operands)


def plan_kernel(tiles, subs, slots, rounds, chunks, fq, rows, width, pair_ref, owner_ref, plan_ref):
    me, me_freq, me_sub = lax.axis_index("tile"), lax.axis_index("freq"), lax.axis_index("sub")
    freqs = lax.axis_size("freq")
    zero = jnp.int32(0)

    def bit(block):
        return jnp.left_shift(jnp.int32(1), block)

    def own(tile):
        return ((1 << subs) - 1) << (subs * tile)

    def up_to(tile):
        return (1 << (subs * (tile + 1))) - 1

    def pick(index, values):
        chosen = zero
        for key, value in values.items():
            chosen = jnp.where(index == key, value, chosen)
        return chosen

    def lowest(bits):
        return jnp.bitwise_and(bits, -bits)

    every = [[zero] * slots for _ in range(tiles)]
    rows_bit, cols_bit, filled = {}, {}, {}
    for k in range(slots):
        rows_bit[k], cols_bit[k], filled[k] = zero, zero, zero
        for t in range(tiles):
            pair = owner_ref[k, t]
            there = pair >= 0
            first = jnp.where(there, bit(pair_ref[0, jnp.maximum(pair, 0)]), 0)
            second = jnp.where(there, bit(pair_ref[1, jnp.maximum(pair, 0)]), 0)
            every[t][k] = first | second
            mine = me == t
            rows_bit[k] = jnp.where(mine, first, rows_bit[k])
            cols_bit[k] = jnp.where(mine, second, cols_bit[k])
            filled[k] = jnp.where(mine, there.astype(jnp.int32), filled[k])
    need = [functools.reduce(jnp.bitwise_or, every[t]) for t in range(tiles)]
    left_to_do = {}
    for t in range(tiles - 1):
        left_to_do[(1, t)] = functools.reduce(jnp.bitwise_or, need[t + 1 :]) & up_to(t)
        left_to_do[(-1, t + 1)] = functools.reduce(jnp.bitwise_or, need[: t + 1]) & ~up_to(t)
    todo = list(need)
    have = [jnp.int32(own(t)) for t in range(tiles)]
    places = [(bit(subs * me + me_sub), 0), (bit(subs * me + 1 - me_sub), 1)]

    def place(block_bit):
        where = jnp.int32(-1)
        for held_bit, index in places:
            where = jnp.where(jnp.logical_and(block_bit == held_bit, block_bit != 0), index, where)
        return where

    needed_rounds = jnp.int32(1)
    my_order = []
    for r in range(rounds):
        sel, over_freq = {}, {}
        for (step, t), want in left_to_do.items():
            cand = have[t] & want
            chosen = zero
            for u in range(tiles - 1, t, -1) if step > 0 else range(0, t):
                chosen = jnp.where(chosen == 0, lowest(cand & need[u]), chosen)
            sel[(step, t)] = chosen
        for t in range(tiles):
            ready = have[t] & todo[t]
            early = ready & every[t][0]
            over_freq[t] = jnp.where(early != 0, lowest(early), lowest(ready))
        for key in sel:
            left_to_do[key] = left_to_do[key] & ~sel[key]
        for t in range(tiles):
            todo[t] = todo[t] & ~over_freq[t]
            for step in (1, -1):
                if (step, t - step) in sel:
                    have[t] = have[t] | sel[(step, t - step)]
        plan_ref[3 * r] = place(pick(me, {t: sel[(1, t)] for t in range(tiles - 1)}))
        plan_ref[3 * r + 1] = place(pick(me, {t: sel[(-1, t)] for t in range(1, tiles)}))
        mine = pick(me, over_freq)
        plan_ref[3 * r + 2] = place(mine)
        my_order.append(mine)
        places.append((pick(me, {t + 1: sel[(1, t)] for t in range(tiles - 1)}), 2 + 2 * r))
        places.append((pick(me, {t - 1: sel[(-1, t)] for t in range(1, tiles)}), 3 + 2 * r))
        rest = functools.reduce(jnp.bitwise_or, todo)
        needed_rounds = needed_rounds + (rest != 0).astype(jnp.int32)
    plan_ref[3 * rounds] = needed_rounds
    base = 3 * rounds + 1
    plan_ref[base] = lax.rem(width - (me_sub * freqs + me_freq) * rows, width)
    n = 0
    for f, s in ((0, 0), (1, 0), (0, 1), (1, 1)):
        share = (me_freq ^ f) * subs + (me_sub ^ s)
        for c in range(chunks):
            plan_ref[base + 1 + n] = share * fq + c * (fq // chunks)
            n += 1
    for k in range(slots):
        for which, wanted in ((0, rows_bit[k]), (1, cols_bit[k])):
            at = zero
            for r in range(rounds):
                at = jnp.where(my_order[r] == wanted, r, at)
            plan_ref[base + 1 + n + 3 * k + which] = at
        plan_ref[base + 1 + n + 3 * k + 2] = filled[k]


def make_plan(pair_list, owner_slots, rounds, chunks, fq, rows, width):
    tiles, slots = owner_slots.shape
    smem = pl.BlockSpec(memory_space=pltpu.SMEM)
    return pl.pallas_call(
        functools.partial(plan_kernel, tiles, lax.axis_size("sub"), slots, rounds, chunks, fq, rows, width),
        in_specs=[smem, smem],
        out_specs=smem,
        out_shape=jax.ShapeDtypeStruct((3 * rounds + 2 + 4 * chunks + 3 * slots,), jnp.int32),
        name="make_plan",
    )(pair_list.T, owner_slots.T)


def choose_kernel(which, chunk, spans, unread, plan, *refs):
    count = len(which)
    held, outs = refs[: len(spans)], refs[len(spans) + unread : len(spans) + unread + count]
    stage, in_sems, out_sems = refs[len(spans) + unread + count :]
    depth = stage.shape[1]

    def load(i, n):
        src = held[n].at[pl.ds(chunk * depth, depth)] if spans[n] else held[n]
        return pltpu.make_async_copy(src, stage.at[i], in_sems.at[i])

    def store(i):
        return pltpu.make_async_copy(stage.at[i], outs[i], out_sems.at[i])

    for i, entry in enumerate(which):
        for n in range(len(spans)):

            @pl.when(plan[entry] == n)
            def _():
                load(i, n).start()

    for i, entry in enumerate(which):

        @pl.when(plan[entry] >= 0)
        def _():
            load(i, 0).wait()
            store(i).start()

    for i, entry in enumerate(which):

        @pl.when(plan[entry] >= 0)
        def _():
            store(i).wait()


def choose(plan, which, held, after, chunk, depth):
    spans = [a.shape[0] != depth for a in held]
    any_spec = pl.BlockSpec(memory_space=pl.ANY)
    out = jax.ShapeDtypeStruct((depth,) + held[0].shape[1:], jnp.float32)
    return pl.pallas_call(
        functools.partial(choose_kernel, which, chunk, spans, len(after)),
        in_specs=[pl.BlockSpec(memory_space=pltpu.SMEM)] + [any_spec] * (len(held) + len(after)),
        out_specs=[any_spec] * len(which),
        out_shape=[out] * len(which),
        scratch_shapes=[
            pltpu.VMEM((len(which),) + out.shape, jnp.float32),
            pltpu.SemaphoreType.DMA((len(which),)),
            pltpu.SemaphoreType.DMA((len(which),)),
        ],
        compiler_params=pltpu.CompilerParams(vmem_limit_bytes=VMEM_LIMIT),
        cost_estimate=pl.CostEstimate(flops=0, bytes_accessed=len(which) * 2 * depth * 32 * 512, transcendentals=0),
        name="choose",
    )(plan, *held, *after)


def relay_kernel(count, *refs):
    srcs, outs = refs[:count], refs[-count - 3 : -3]
    stage, in_sems, out_sems = refs[-3:]
    loads = [pltpu.make_async_copy(srcs[i], stage.at[i], in_sems.at[i]) for i in range(count)]
    stores = [pltpu.make_async_copy(stage.at[i], outs[i], out_sems.at[i]) for i in range(count)]
    for load in loads:
        load.start()
    for load, store in zip(loads, stores):
        load.wait()
        store.start()
    for store in stores:
        store.wait()


def relay(arrays, after):
    count = len(arrays)
    any_spec = pl.BlockSpec(memory_space=pl.ANY)
    return pl.pallas_call(
        functools.partial(relay_kernel, count),
        in_specs=[any_spec] * (count + 1),
        out_specs=[any_spec] * count,
        out_shape=[jax.ShapeDtypeStruct(a.shape, a.dtype) for a in arrays],
        scratch_shapes=[
            pltpu.VMEM((count,) + arrays[0].shape, jnp.float32),
            pltpu.SemaphoreType.DMA((count,)),
            pltpu.SemaphoreType.DMA((count,)),
        ],
        compiler_params=pltpu.CompilerParams(vmem_limit_bytes=VMEM_LIMIT),
        cost_estimate=pl.CostEstimate(flops=0, bytes_accessed=count * 2**20, transcendentals=0),
        name="relay",
    )(*arrays, after)


ROUNDS = 6
CHUNKS = 2


def gather_all(slots, rows, windows, mine, passed, pair_list, owner_slots):
    freq_parts, subs = lax.axis_size("freq"), lax.axis_size("sub")
    me_tile, me_freq, me_sub = lax.axis_index("tile"), lax.axis_index("freq"), lax.axis_index("sub")
    fq, _, width = mine.shape
    nq = freq_parts * subs
    my_pairs = lax.dynamic_index_in_dim(owner_slots, me_tile, 0, keepdims=False)
    filled = (my_pairs >= 0).astype(jnp.int32)
    wanted = jnp.take(pair_list, jnp.maximum(my_pairs, 0), axis=0)
    shift = (width - (me_sub * freq_parts + me_freq) * rows) % width
    held = lax.all_gather(jnp.stack([mine, passed]), "tile")
    items = []
    for slot in range(slots):
        for which in range(2):
            block = wanted[slot, which]
            chosen = held[block // 2, (block % 2) ^ me_sub]
            items.append(lax.all_gather(chosen, ("freq", "sub")))
    srcs = [[item[q] for item in items] for q in range(nq)]
    first = jnp.arange(nq, dtype=jnp.int32) * fq
    meta = jnp.concatenate(
        [shift.reshape(1), first]
        + [jnp.stack([jnp.int32(2 * k), jnp.int32(2 * k + 1), filled[k]]) for k in range(slots)]
    ).astype(jnp.int32)
    return correlate(meta, 0, srcs, rows, slots, windows)


def in_rounds(count, slots, rows, windows, mine, passed, plan):
    tiles = lax.axis_size("tile")
    right = [(t, t + 1) for t in range(tiles - 1)]
    left = [(t + 1, t) for t in range(tiles - 1)]
    swap = [(0, 1), (1, 0)]
    depth = mine.shape[0] // CHUNKS
    held = [[mine, passed] for _ in range(CHUNKS)]
    srcs = [[] for _ in range(4 * CHUNKS)]
    for r in range(count):
        for c in range(CHUNKS):
            after = [srcs[n * CHUNKS + c][r - age] for n, age in ((1, 1), (2, 1), (3, 2)) if r >= age]
            if r < count - 1:
                to_right, to_left, to_freq = choose(plan, (3 * r, 3 * r + 1, 3 * r + 2), held[c], after, c, depth)
                held[c] = held[c] + [lax.ppermute(to_right, "tile", right), lax.ppermute(to_left, "tile", left)]
            else:
                (to_freq,) = choose(plan, (3 * r + 2,), held[c], after, c, depth)
            crossed = lax.ppermute(to_freq, "freq", swap)
            srcs[c].append(to_freq)
            srcs[CHUNKS + c].append(crossed)
            srcs[2 * CHUNKS + c].append(lax.ppermute(to_freq, "sub", swap))
            if r < count - 1:
                srcs[3 * CHUNKS + c].append(lax.ppermute(crossed, "sub", swap))
    base = 3 * ROUNDS + 1
    before = [share[: count - 1] for share in srcs]
    sent = [share[-1] for share in srcs[:CHUNKS]]
    first = correlate(plan, base, before, rows, slots, windows, count - 1, False, sent)
    for c, copied in enumerate(relay([share[-1] for share in srcs[CHUNKS : 2 * CHUNKS]], first)):
        srcs[3 * CHUNKS + c].append(lax.ppermute(copied, "sub", swap))
    return correlate(plan, base, srcs, rows, slots, windows, count - 1, True, (), first)


def body(spectra, pair_list, owner_slots):
    tiles, freq_parts, subs = lax.axis_size("tile"), lax.axis_size("freq"), lax.axis_size("sub")
    _, windows, band, width = spectra.shape
    slots = owner_slots.shape[1]
    fq = band // subs
    rows = width // (freq_parts * subs)
    me_sub = lax.axis_index("sub")
    other = whiten(spectra, 1 - me_sub, fq)
    passed = lax.ppermute(other, "sub", [(0, 1), (1, 0)])
    mine = whiten(spectra, me_sub, fq)
    whole = functools.partial(gather_all, slots, rows, windows)
    if freq_parts != 2 or tiles > 4:
        return whole(mine, passed, pair_list, owner_slots)
    plan = make_plan(pair_list, owner_slots, ROUNDS, CHUNKS, fq, rows, width)
    branches = [
        functools.partial(lambda n, a, b, p, pairs, owners: in_rounds(n, slots, rows, windows, a, b, p), n)
        for n in range(2, ROUNDS + 1)
    ]
    branches.append(lambda a, b, p, pairs, owners: whole(a, b, pairs, owners))
    return lax.switch(
        jnp.maximum(plan[3 * ROUNDS], 2) - 2, branches, mine, passed, plan, pair_list, owner_slots
    )


def solution(mesh):
    in_specs = (P("day", None, "freq", ("tile", "sub")), P(), P())
    out_specs = P(("sub", "freq"), ("day", "tile"), None, None)
    return jax.shard_map(body, mesh=mesh, in_specs=in_specs, out_specs=out_specs, check_vma=False)
```

```python
import functools
import math

import jax
import jax.numpy as jnp
import ml_dtypes
import numpy as np
from jax import lax
from jax.experimental import pallas as pl
from jax.experimental.pallas import tpu as pltpu
from jax.sharding import PartitionSpec as P

FREQS = 256
LAGS = 256
BF16 = jnp.bfloat16
VMEM_LIMIT = 56 * 1024 * 1024
UNROLL = 4
OUT_ROWS = 8


def lag_tables(scale):
    lag_ids = np.arange(LAGS) - LAGS // 2
    phases = (lag_ids[:, None] * np.arange(FREQS)[None, :]) % (2 * FREQS)
    angles = phases * (np.pi / FREQS)
    table = np.concatenate([np.cos(angles), -np.sin(angles)], axis=1) * scale
    head = table.astype(ml_dtypes.bfloat16)
    tail = (table - head.astype(np.float64)).astype(ml_dtypes.bfloat16)
    return np.concatenate([head, tail], axis=0)


def split(x):
    head = x.astype(BF16)
    return head, (x - head.astype(jnp.float32)).astype(BF16)


def whiten_kernel(part_ref, x_ref, o_ref):
    windows = x_ref.shape[1]
    re, im = x_ref[0], x_ref[1]
    power = re * re + im * im
    scale = jnp.where(power > 1.0, lax.rsqrt(power), 1.0)
    o_ref[:, :windows, :] = jnp.swapaxes(re * scale, 0, 1)
    o_ref[:, windows:, :] = jnp.swapaxes(im * scale, 0, 1)


def whiten(spectra, part, fq):
    parts, windows, _, width = spectra.shape
    chunk = min(32, fq)
    steps = fq // chunk
    return pl.pallas_call(
        whiten_kernel,
        grid_spec=pltpu.PrefetchScalarGridSpec(
            num_scalar_prefetch=1,
            grid=(steps,),
            in_specs=[pl.BlockSpec((parts, windows, chunk, width), lambda i, p: (0, 0, p[0] * steps + i, 0))],
            out_specs=pl.BlockSpec((chunk, parts * windows, width), lambda i, p: (i, 0, 0)),
        ),
        out_shape=jax.ShapeDtypeStruct((fq, parts * windows, width), jnp.float32),
        compiler_params=pltpu.CompilerParams(vmem_limit_bytes=VMEM_LIMIT),
        cost_estimate=pl.CostEstimate(flops=fq * 32 * width * 8, bytes_accessed=fq * 32 * width * 8, transcendentals=0),
        name="whiten",
    )(part.reshape(1), spectra)


def corr_kernel(base, nq, items, rows, slots, early, late, unread, meta, *refs):
    srcs = refs[: nq * items]
    table, mask = refs[nq * items : nq * items + 2]
    out, row_buf, col_buf, cross, out_buf, in_sem, out_sem = refs[nq * items + 2 + unread + (late is True) :]
    fq, kw, width = row_buf.shape[2:]
    group = 4
    packs = width // rows
    per_pack = group * packs
    m_rows = group * 2 * rows
    out_rows = out_buf.shape[1]

    def entry(slot, n):
        return meta[base + 1 + nq + 3 * slot + n]

    def in_turn(slot):
        filled = entry(slot, 2) > 0
        if late is None:
            return filled
        ready = jnp.maximum(entry(slot, 0), entry(slot, 1)) < early
        return jnp.logical_and(filled, jnp.logical_not(ready) if late else ready)

    def fetch(slot):
        for which, buf in ((0, row_buf), (1, col_buf)):
            item = entry(slot, which)
            for n in range(items):

                @pl.when(jnp.logical_and(item == n, in_turn(slot)))
                def _():
                    for q in range(nq):
                        pltpu.make_async_copy(srcs[q * items + n], buf.at[slot, q], in_sem.at[slot, which, q]).start()

    def wait_fetch(slot, q):
        for which, buf in ((0, row_buf), (1, col_buf)):
            pltpu.make_async_copy(srcs[0], buf.at[slot, q], in_sem.at[slot, which, q]).wait()

    def out_copy(slot, step, buf):
        return pltpu.make_async_copy(out_buf.at[buf], out.at[pl.ds(step * out_rows, out_rows), slot], out_sem.at[buf])

    @pl.loop(0, slots)
    def _(slot):
        fetch(slot)

    per_share = fq // per_pack
    together = max(1, UNROLL // per_share)
    lane = lax.broadcasted_iota(jnp.int32, (width, width), 1)

    def cross_pack(slot, q, p):
        packed = jnp.zeros((width, width), jnp.float32)
        for g in range(packs):
            part = row_buf[slot, q, pl.ds(p * per_pack + g * group, group)].reshape(group * kw, width)
            shift = lax.rem(meta[base] + g * rows, width)
            packed = jnp.where(lane // rows == g, pltpu.roll(part, shift, 1), packed)
        turned = packed.T
        swapped = jnp.where(
            lane % kw < kw // 2, pltpu.roll(turned, width - kw // 2, 1), -pltpu.roll(turned, kw // 2, 1)
        )
        for g in range(packs):
            span = slice(g * rows, (g + 1) * rows)
            head, tail = split(jnp.concatenate([turned[span], swapped[span]], axis=0))
            left = jnp.concatenate(
                [jnp.concatenate([head * mask[n], tail * mask[n]], axis=1) for n in range(group)], axis=0
            )
            part = col_buf[slot, q, pl.ds(p * per_pack + g * group, group)].reshape(group * kw, width)
            top = jnp.concatenate(split(part), axis=1)
            both = jnp.dot(left, jnp.concatenate([top, top], axis=0), preferred_element_type=jnp.float32)
            first = (meta[base + 1 + q] + p * per_pack + g * group) * (2 * rows)
            cross[pl.ds(pl.multiple_of(first, m_rows), m_rows)] = both[:, :width] + both[:, width:]

    def lag_step(slot, step, buf):
        for pair in range(out_rows // 2):
            halves = [
                jnp.concatenate(
                    [
                        cross[pl.ds(e * rows + step * out_rows + pair * 2 + n, FREQS, stride=2 * rows)]
                        for n in range(2)
                    ],
                    axis=1,
                )
                for e in range(2)
            ]
            head, tail = split(jnp.concatenate(halves, axis=0))
            high = jnp.dot(table[...], head, preferred_element_type=jnp.float32)
            low = jnp.dot(table[:LAGS], tail, preferred_element_type=jnp.float32)
            lagged = high[:LAGS] + high[LAGS:] + low
            for n in range(2):
                out_buf[buf, pair * 2 + n] = lagged[:, n * width : (n + 1) * width]

    steps = rows // out_rows
    @pl.loop(0, slots)
    def _(slot):
        @pl.when(in_turn(slot))
        def _():
            @pl.loop(0, nq // together)
            def _(i):
                for n in range(together):
                    wait_fetch(slot, i * together + n)
                for n in range(together):
                    for p in range(per_share):
                        cross_pack(slot, i * together + n, p)

            @pl.loop(0, steps)
            def _(step):
                buf = lax.rem(step, 2)

                @pl.when(step >= 2)
                def _():
                    out_copy(slot, step, buf).wait()

                lag_step(slot, step, buf)
                out_copy(slot, step, buf).start()

            for buf in range(2):
                out_copy(slot, 0, buf).wait()

        if not late:

            @pl.when(entry(slot, 2) == 0)
            def _():
                out_buf[0] = jnp.zeros(out_buf.shape[1:], jnp.float32)
                for step in range(steps):
                    out_copy(slot, step, 0).start()
                for step in range(steps):
                    out_copy(slot, step, 0).wait()


def correlate(meta, base, srcs, rows, slots, windows, early=0, late=None, after=(), into=None):
    nq, items = len(srcs), len(srcs[0])
    fq, kw, width = srcs[0][0].shape
    table = jnp.asarray(lag_tables(1.0 / math.sqrt(windows * FREQS)))
    mask_np = np.broadcast_to((np.arange(width)[None, None, :] // kw) == np.arange(4)[:, None, None], (4, 2 * rows, width))
    mask = jnp.asarray(mask_np.astype(ml_dtypes.bfloat16))
    any_spec = pl.BlockSpec(memory_space=pl.ANY)
    vmem_spec = pl.BlockSpec(memory_space=pltpu.VMEM)
    operands = [meta, *[a for share in srcs for a in share], table, mask, *after]
    in_specs = [pl.BlockSpec(memory_space=pltpu.SMEM)] + [any_spec] * (nq * items)
    in_specs += [vmem_spec] * 2 + [any_spec] * len(after)
    aliases = {}
    if into is not None:
        aliases = {len(operands): 0}
        operands.append(into)
        in_specs.append(any_spec)
    return pl.pallas_call(
        functools.partial(corr_kernel, base, nq, items, rows, slots, early, late, len(after)),
        in_specs=in_specs,
        out_specs=any_spec,
        out_shape=jax.ShapeDtypeStruct((rows, slots, LAGS, width), jnp.float32),
        scratch_shapes=[
            pltpu.VMEM((slots, nq, fq, kw, width), jnp.float32),
            pltpu.VMEM((slots, nq, fq, kw, width), jnp.float32),
            pltpu.VMEM((FREQS * 2 * rows, width), jnp.float32),
            pltpu.VMEM((2, OUT_ROWS, LAGS, width), jnp.float32),
            pltpu.SemaphoreType.DMA((slots, 2, nq)),
            pltpu.SemaphoreType.DMA((2,)),
        ],
        input_output_aliases=aliases,
        compiler_params=pltpu.CompilerParams(vmem_limit_bytes=VMEM_LIMIT),
        cost_estimate=pl.CostEstimate(
            flops=2 * slots * rows * LAGS * 2 * FREQS * width * 6, bytes_accessed=24 * 1024 * 1024, transcendentals=0
        ),
        name="correlate",
    )(*operands)


def plan_kernel(tiles, subs, slots, rounds, chunks, fq, rows, width, pair_ref, owner_ref, plan_ref):
    me, me_freq, me_sub = lax.axis_index("tile"), lax.axis_index("freq"), lax.axis_index("sub")
    freqs = lax.axis_size("freq")
    zero = jnp.int32(0)

    def bit(block):
        return jnp.left_shift(jnp.int32(1), block)

    def own(tile):
        return ((1 << subs) - 1) << (subs * tile)

    def up_to(tile):
        return (1 << (subs * (tile + 1))) - 1

    def pick(index, values):
        chosen = zero
        for key, value in values.items():
            chosen = jnp.where(index == key, value, chosen)
        return chosen

    def lowest(bits):
        return jnp.bitwise_and(bits, -bits)

    every = [[zero] * slots for _ in range(tiles)]
    rows_bit, cols_bit, filled = {}, {}, {}
    for k in range(slots):
        rows_bit[k], cols_bit[k], filled[k] = zero, zero, zero
        for t in range(tiles):
            pair = owner_ref[k, t]
            there = pair >= 0
            first = jnp.where(there, bit(pair_ref[0, jnp.maximum(pair, 0)]), 0)
            second = jnp.where(there, bit(pair_ref[1, jnp.maximum(pair, 0)]), 0)
            every[t][k] = first | second
            mine = me == t
            rows_bit[k] = jnp.where(mine, first, rows_bit[k])
            cols_bit[k] = jnp.where(mine, second, cols_bit[k])
            filled[k] = jnp.where(mine, there.astype(jnp.int32), filled[k])
    need = [functools.reduce(jnp.bitwise_or, every[t]) for t in range(tiles)]
    left_to_do = {}
    for t in range(tiles - 1):
        left_to_do[(1, t)] = functools.reduce(jnp.bitwise_or, need[t + 1 :]) & up_to(t)
        left_to_do[(-1, t + 1)] = functools.reduce(jnp.bitwise_or, need[: t + 1]) & ~up_to(t)
    todo = list(need)
    have = [jnp.int32(own(t)) for t in range(tiles)]
    places = [(bit(subs * me + me_sub), 0), (bit(subs * me + 1 - me_sub), 1)]

    def place(block_bit):
        where = jnp.int32(-1)
        for held_bit, index in places:
            where = jnp.where(jnp.logical_and(block_bit == held_bit, block_bit != 0), index, where)
        return where

    needed_rounds = jnp.int32(1)
    my_order = []
    for r in range(rounds):
        sel, over_freq = {}, {}
        for (step, t), want in left_to_do.items():
            cand = have[t] & want
            chosen = zero
            for u in range(tiles - 1, t, -1) if step > 0 else range(0, t):
                chosen = jnp.where(chosen == 0, lowest(cand & need[u]), chosen)
            sel[(step, t)] = chosen
        for t in range(tiles):
            ready = have[t] & todo[t]
            early = ready & every[t][0]
            over_freq[t] = jnp.where(early != 0, lowest(early), lowest(ready))
        for key in sel:
            left_to_do[key] = left_to_do[key] & ~sel[key]
        for t in range(tiles):
            todo[t] = todo[t] & ~over_freq[t]
            for step in (1, -1):
                if (step, t - step) in sel:
                    have[t] = have[t] | sel[(step, t - step)]
        plan_ref[3 * r] = place(pick(me, {t: sel[(1, t)] for t in range(tiles - 1)}))
        plan_ref[3 * r + 1] = place(pick(me, {t: sel[(-1, t)] for t in range(1, tiles)}))
        mine = pick(me, over_freq)
        plan_ref[3 * r + 2] = place(mine)
        my_order.append(mine)
        places.append((pick(me, {t + 1: sel[(1, t)] for t in range(tiles - 1)}), 2 + 2 * r))
        places.append((pick(me, {t - 1: sel[(-1, t)] for t in range(1, tiles)}), 3 + 2 * r))
        rest = functools.reduce(jnp.bitwise_or, todo)
        needed_rounds = needed_rounds + (rest != 0).astype(jnp.int32)
    plan_ref[3 * rounds] = needed_rounds
    base = 3 * rounds + 1
    plan_ref[base] = lax.rem(width - (me_sub * freqs + me_freq) * rows, width)
    n = 0
    for f, s in ((0, 0), (1, 0), (0, 1), (1, 1)):
        share = (me_freq ^ f) * subs + (me_sub ^ s)
        for c in range(chunks):
            plan_ref[base + 1 + n] = share * fq + c * (fq // chunks)
            n += 1
    for k in range(slots):
        for which, wanted in ((0, rows_bit[k]), (1, cols_bit[k])):
            at = zero
            for r in range(rounds):
                at = jnp.where(my_order[r] == wanted, r, at)
            plan_ref[base + 1 + n + 3 * k + which] = at
        plan_ref[base + 1 + n + 3 * k + 2] = filled[k]


def make_plan(pair_list, owner_slots, rounds, chunks, fq, rows, width):
    tiles, slots = owner_slots.shape
    smem = pl.BlockSpec(memory_space=pltpu.SMEM)
    return pl.pallas_call(
        functools.partial(plan_kernel, tiles, lax.axis_size("sub"), slots, rounds, chunks, fq, rows, width),
        in_specs=[smem, smem],
        out_specs=smem,
        out_shape=jax.ShapeDtypeStruct((3 * rounds + 2 + 4 * chunks + 3 * slots,), jnp.int32),
        name="make_plan",
    )(pair_list.T, owner_slots.T)


def choose_kernel(which, chunk, spans, unread, plan, *refs):
    count = len(which)
    held, outs = refs[: len(spans)], refs[len(spans) + unread : len(spans) + unread + count]
    stage, in_sems, out_sems = refs[len(spans) + unread + count :]
    depth = stage.shape[1]

    def load(i, n):
        src = held[n].at[pl.ds(chunk * depth, depth)] if spans[n] else held[n]
        return pltpu.make_async_copy(src, stage.at[i], in_sems.at[i])

    def store(i):
        return pltpu.make_async_copy(stage.at[i], outs[i], out_sems.at[i])

    for i, entry in enumerate(which):
        for n in range(len(spans)):

            @pl.when(plan[entry] == n)
            def _():
                load(i, n).start()

    for i, entry in enumerate(which):

        @pl.when(plan[entry] >= 0)
        def _():
            load(i, 0).wait()
            store(i).start()

    for i, entry in enumerate(which):

        @pl.when(plan[entry] >= 0)
        def _():
            store(i).wait()


def choose(plan, which, held, after, chunk, depth):
    spans = [a.shape[0] != depth for a in held]
    any_spec = pl.BlockSpec(memory_space=pl.ANY)
    out = jax.ShapeDtypeStruct((depth,) + held[0].shape[1:], jnp.float32)
    return pl.pallas_call(
        functools.partial(choose_kernel, which, chunk, spans, len(after)),
        in_specs=[pl.BlockSpec(memory_space=pltpu.SMEM)] + [any_spec] * (len(held) + len(after)),
        out_specs=[any_spec] * len(which),
        out_shape=[out] * len(which),
        scratch_shapes=[
            pltpu.VMEM((len(which),) + out.shape, jnp.float32),
            pltpu.SemaphoreType.DMA((len(which),)),
            pltpu.SemaphoreType.DMA((len(which),)),
        ],
        compiler_params=pltpu.CompilerParams(vmem_limit_bytes=VMEM_LIMIT),
        cost_estimate=pl.CostEstimate(flops=0, bytes_accessed=len(which) * 2 * depth * 32 * 512, transcendentals=0),
        name="choose",
    )(plan, *held, *after)


def relay_kernel(count, *refs):
    srcs, outs = refs[:count], refs[-count - 3 : -3]
    stage, in_sems, out_sems = refs[-3:]
    loads = [pltpu.make_async_copy(srcs[i], stage.at[i], in_sems.at[i]) for i in range(count)]
    stores = [pltpu.make_async_copy(stage.at[i], outs[i], out_sems.at[i]) for i in range(count)]
    for load in loads:
        load.start()
    for load, store in zip(loads, stores):
        load.wait()
        store.start()
    for store in stores:
        store.wait()


def relay(arrays, after):
    count = len(arrays)
    any_spec = pl.BlockSpec(memory_space=pl.ANY)
    return pl.pallas_call(
        functools.partial(relay_kernel, count),
        in_specs=[any_spec] * (count + 1),
        out_specs=[any_spec] * count,
        out_shape=[jax.ShapeDtypeStruct(a.shape, a.dtype) for a in arrays],
        scratch_shapes=[
            pltpu.VMEM((count,) + arrays[0].shape, jnp.float32),
            pltpu.SemaphoreType.DMA((count,)),
            pltpu.SemaphoreType.DMA((count,)),
        ],
        compiler_params=pltpu.CompilerParams(vmem_limit_bytes=VMEM_LIMIT),
        cost_estimate=pl.CostEstimate(flops=0, bytes_accessed=count * 2**20, transcendentals=0),
        name="relay",
    )(*arrays, after)


FEWEST, ROUNDS = 3, 5
CHUNKS = 2


def gather_all(slots, rows, windows, mine, passed, pair_list, owner_slots):
    freq_parts, subs = lax.axis_size("freq"), lax.axis_size("sub")
    me_tile, me_freq, me_sub = lax.axis_index("tile"), lax.axis_index("freq"), lax.axis_index("sub")
    fq, _, width = mine.shape
    nq = freq_parts * subs
    my_pairs = lax.dynamic_index_in_dim(owner_slots, me_tile, 0, keepdims=False)
    filled = (my_pairs >= 0).astype(jnp.int32)
    wanted = jnp.take(pair_list, jnp.maximum(my_pairs, 0), axis=0)
    shift = (width - (me_sub * freq_parts + me_freq) * rows) % width
    held = lax.all_gather(jnp.stack([mine, passed]), "tile")
    items = []
    for slot in range(slots):
        for which in range(2):
            block = wanted[slot, which]
            chosen = held[block // 2, (block % 2) ^ me_sub]
            items.append(lax.all_gather(chosen, ("freq", "sub")))
    srcs = [[item[q] for item in items] for q in range(nq)]
    first = jnp.arange(nq, dtype=jnp.int32) * fq
    meta = jnp.concatenate(
        [shift.reshape(1), first]
        + [jnp.stack([jnp.int32(2 * k), jnp.int32(2 * k + 1), filled[k]]) for k in range(slots)]
    ).astype(jnp.int32)
    return correlate(meta, 0, srcs, rows, slots, windows)


def in_rounds(count, slots, rows, windows, mine, passed, plan):
    tiles = lax.axis_size("tile")
    right = [(t, t + 1) for t in range(tiles - 1)]
    left = [(t + 1, t) for t in range(tiles - 1)]
    swap = [(0, 1), (1, 0)]
    depth = mine.shape[0] // CHUNKS
    held = [[mine, passed] for _ in range(CHUNKS)]
    srcs = [[] for _ in range(4 * CHUNKS)]
    for r in range(count):
        for c in range(CHUNKS):
            after = [srcs[n * CHUNKS + c][r - age] for n, age in ((1, 1), (2, 1), (3, 2)) if r >= age]
            if r < count - 1:
                to_right, to_left, to_freq = choose(plan, (3 * r, 3 * r + 1, 3 * r + 2), held[c], after, c, depth)
                held[c] = held[c] + [lax.ppermute(to_right, "tile", right), lax.ppermute(to_left, "tile", left)]
            else:
                (to_freq,) = choose(plan, (3 * r + 2,), held[c], after, c, depth)
            crossed = lax.ppermute(to_freq, "freq", swap)
            srcs[c].append(to_freq)
            srcs[CHUNKS + c].append(crossed)
            srcs[2 * CHUNKS + c].append(lax.ppermute(to_freq, "sub", swap))
            if r < count - 1:
                srcs[3 * CHUNKS + c].append(lax.ppermute(crossed, "sub", swap))
    base = 3 * ROUNDS + 1
    before = [share[: count - 1] for share in srcs]
    sent = [share[-1] for share in srcs[:CHUNKS]]
    first = correlate(plan, base, before, rows, slots, windows, count - 1, False, sent)
    for c, copied in enumerate(relay([share[-1] for share in srcs[CHUNKS : 2 * CHUNKS]], first)):
        srcs[3 * CHUNKS + c].append(lax.ppermute(copied, "sub", swap))
    return correlate(plan, base, srcs, rows, slots, windows, count - 1, True, (), first)


def body(spectra, pair_list, owner_slots):
    tiles, freq_parts, subs = lax.axis_size("tile"), lax.axis_size("freq"), lax.axis_size("sub")
    _, windows, band, width = spectra.shape
    slots = owner_slots.shape[1]
    fq = band // subs
    rows = width // (freq_parts * subs)
    me_sub = lax.axis_index("sub")
    other = whiten(spectra, 1 - me_sub, fq)
    passed = lax.ppermute(other, "sub", [(0, 1), (1, 0)])
    mine = whiten(spectra, me_sub, fq)
    whole = functools.partial(gather_all, slots, rows, windows)
    if freq_parts != 2 or tiles > 4:
        return whole(mine, passed, pair_list, owner_slots)
    plan = make_plan(pair_list, owner_slots, ROUNDS, CHUNKS, fq, rows, width)
    branches = [
        functools.partial(lambda n, a, b, p, pairs, owners: in_rounds(n, slots, rows, windows, a, b, p), n)
        for n in range(FEWEST, ROUNDS + 1)
    ]
    branches.append(lambda a, b, p, pairs, owners: whole(a, b, pairs, owners))
    return lax.switch(
        jnp.maximum(plan[3 * ROUNDS], FEWEST) - FEWEST, branches, mine, passed, plan, pair_list, owner_slots
    )


def solution(mesh):
    in_specs = (P("day", None, "freq", ("tile", "sub")), P(), P())
    out_specs = P(("sub", "freq"), ("day", "tile"), None, None)
    return jax.shard_map(body, mesh=mesh, in_specs=in_specs, out_specs=out_specs, check_vma=False)
```

```python
import functools
import math

import jax
import jax.numpy as jnp
import ml_dtypes
import numpy as np
from jax import lax
from jax.experimental import pallas as pl
from jax.experimental.pallas import tpu as pltpu
from jax.sharding import PartitionSpec as P

FREQS = 256
LAGS = 256
BF16 = jnp.bfloat16
VMEM_LIMIT = 56 * 1024 * 1024
UNROLL = 4
OUT_ROWS = 8


def lag_tables(scale):
    lag_ids = np.arange(LAGS) - LAGS // 2
    phases = (lag_ids[:, None] * np.arange(FREQS)[None, :]) % (2 * FREQS)
    angles = phases * (np.pi / FREQS)
    table = np.concatenate([np.cos(angles), -np.sin(angles)], axis=1) * scale
    head = table.astype(ml_dtypes.bfloat16)
    tail = (table - head.astype(np.float64)).astype(ml_dtypes.bfloat16)
    return np.concatenate([head, tail], axis=0)


def split(x):
    head = x.astype(BF16)
    return head, (x - head.astype(jnp.float32)).astype(BF16)


def whiten_kernel(part_ref, x_ref, o_ref):
    windows = x_ref.shape[1]
    re, im = x_ref[0], x_ref[1]
    power = re * re + im * im
    scale = jnp.where(power > 1.0, lax.rsqrt(power), 1.0)
    o_ref[:, :windows, :] = jnp.swapaxes(re * scale, 0, 1)
    o_ref[:, windows:, :] = jnp.swapaxes(im * scale, 0, 1)


def whiten(spectra, part, fq):
    parts, windows, _, width = spectra.shape
    chunk = min(32, fq)
    steps = fq // chunk
    return pl.pallas_call(
        whiten_kernel,
        grid_spec=pltpu.PrefetchScalarGridSpec(
            num_scalar_prefetch=1,
            grid=(steps,),
            in_specs=[pl.BlockSpec((parts, windows, chunk, width), lambda i, p: (0, 0, p[0] * steps + i, 0))],
            out_specs=pl.BlockSpec((chunk, parts * windows, width), lambda i, p: (i, 0, 0)),
        ),
        out_shape=jax.ShapeDtypeStruct((fq, parts * windows, width), jnp.float32),
        compiler_params=pltpu.CompilerParams(vmem_limit_bytes=VMEM_LIMIT),
        cost_estimate=pl.CostEstimate(flops=fq * 32 * width * 8, bytes_accessed=fq * 32 * width * 8, transcendentals=0),
        name="whiten",
    )(part.reshape(1), spectra)


def corr_kernel(base, nq, items, rows, slots, early, late, unread, meta, *refs):
    srcs = refs[: nq * items]
    table, mask = refs[nq * items : nq * items + 2]
    out, row_buf, col_buf, cross, out_buf, in_sem, out_sem = refs[nq * items + 2 + unread + (late is True) :]
    fq, kw, width = row_buf.shape[2:]
    group = 4
    packs = width // rows
    per_pack = group * packs
    m_rows = group * 2 * rows
    out_rows = out_buf.shape[1]

    def entry(slot, n):
        return meta[base + 1 + nq + 3 * slot + n]

    def in_turn(slot):
        filled = entry(slot, 2) > 0
        if late is None:
            return filled
        ready = jnp.maximum(entry(slot, 0), entry(slot, 1)) < early
        return jnp.logical_and(filled, jnp.logical_not(ready) if late else ready)

    def fetch(slot):
        for which, buf in ((0, row_buf), (1, col_buf)):
            item = entry(slot, which)
            for n in range(items):

                @pl.when(jnp.logical_and(item == n, in_turn(slot)))
                def _():
                    for q in range(nq):
                        pltpu.make_async_copy(srcs[q * items + n], buf.at[slot, q], in_sem.at[slot, which, q]).start()

    def wait_fetch(slot, q):
        for which, buf in ((0, row_buf), (1, col_buf)):
            pltpu.make_async_copy(srcs[0], buf.at[slot, q], in_sem.at[slot, which, q]).wait()

    def out_copy(slot, step, buf):
        return pltpu.make_async_copy(out_buf.at[buf], out.at[pl.ds(step * out_rows, out_rows), slot], out_sem.at[buf])

    @pl.loop(0, slots)
    def _(slot):
        fetch(slot)

    per_share = fq // per_pack
    together = max(1, UNROLL // per_share)
    lane = lax.broadcasted_iota(jnp.int32, (width, width), 1)

    def cross_pack(slot, q, p):
        packed = jnp.zeros((width, width), jnp.float32)
        for g in range(packs):
            part = row_buf[slot, q, pl.ds(p * per_pack + g * group, group)].reshape(group * kw, width)
            shift = lax.rem(meta[base] + g * rows, width)
            packed = jnp.where(lane // rows == g, pltpu.roll(part, shift, 1), packed)
        turned = packed.T
        swapped = jnp.where(
            lane % kw < kw // 2, pltpu.roll(turned, width - kw // 2, 1), -pltpu.roll(turned, kw // 2, 1)
        )
        for g in range(packs):
            span = slice(g * rows, (g + 1) * rows)
            head, tail = split(jnp.concatenate([turned[span], swapped[span]], axis=0))
            left = jnp.concatenate(
                [jnp.concatenate([head * mask[n], tail * mask[n]], axis=1) for n in range(group)], axis=0
            )
            part = col_buf[slot, q, pl.ds(p * per_pack + g * group, group)].reshape(group * kw, width)
            top = jnp.concatenate(split(part), axis=1)
            both = jnp.dot(left, jnp.concatenate([top, top], axis=0), preferred_element_type=jnp.float32)
            first = (meta[base + 1 + q] + p * per_pack + g * group) * (2 * rows)
            cross[pl.ds(pl.multiple_of(first, m_rows), m_rows)] = both[:, :width] + both[:, width:]

    def lag_step(slot, step, buf):
        for pair in range(out_rows // 2):
            halves = [
                jnp.concatenate(
                    [
                        cross[pl.ds(e * rows + step * out_rows + pair * 2 + n, FREQS, stride=2 * rows)]
                        for n in range(2)
                    ],
                    axis=1,
                )
                for e in range(2)
            ]
            head, tail = split(jnp.concatenate(halves, axis=0))
            high = jnp.dot(table[...], head, preferred_element_type=jnp.float32)
            low = jnp.dot(table[:LAGS], tail, preferred_element_type=jnp.float32)
            lagged = high[:LAGS] + high[LAGS:] + low
            for n in range(2):
                out_buf[buf, pair * 2 + n] = lagged[:, n * width : (n + 1) * width]

    steps = rows // out_rows
    @pl.loop(0, slots)
    def _(slot):
        @pl.when(in_turn(slot))
        def _():
            @pl.loop(0, nq // together)
            def _(i):
                for n in range(together):
                    wait_fetch(slot, i * together + n)
                for n in range(together):
                    for p in range(per_share):
                        cross_pack(slot, i * together + n, p)

            @pl.loop(0, steps)
            def _(step):
                buf = lax.rem(step, 2)

                @pl.when(step >= 2)
                def _():
                    out_copy(slot, step, buf).wait()

                lag_step(slot, step, buf)
                out_copy(slot, step, buf).start()

            for buf in range(2):
                out_copy(slot, 0, buf).wait()

        if not late:

            @pl.when(entry(slot, 2) == 0)
            def _():
                out_buf[0] = jnp.zeros(out_buf.shape[1:], jnp.float32)
                for step in range(steps):
                    out_copy(slot, step, 0).start()
                for step in range(steps):
                    out_copy(slot, step, 0).wait()


def correlate(meta, base, srcs, rows, slots, windows, early=0, late=None, after=(), into=None):
    nq, items = len(srcs), len(srcs[0])
    fq, kw, width = srcs[0][0].shape
    table = jnp.asarray(lag_tables(1.0 / math.sqrt(windows * FREQS)))
    mask_np = np.broadcast_to((np.arange(width)[None, None, :] // kw) == np.arange(4)[:, None, None], (4, 2 * rows, width))
    mask = jnp.asarray(mask_np.astype(ml_dtypes.bfloat16))
    any_spec = pl.BlockSpec(memory_space=pl.ANY)
    vmem_spec = pl.BlockSpec(memory_space=pltpu.VMEM)
    operands = [meta, *[a for share in srcs for a in share], table, mask, *after]
    in_specs = [pl.BlockSpec(memory_space=pltpu.SMEM)] + [any_spec] * (nq * items)
    in_specs += [vmem_spec] * 2 + [any_spec] * len(after)
    aliases = {}
    if into is not None:
        aliases = {len(operands): 0}
        operands.append(into)
        in_specs.append(any_spec)
    return pl.pallas_call(
        functools.partial(corr_kernel, base, nq, items, rows, slots, early, late, len(after)),
        in_specs=in_specs,
        out_specs=any_spec,
        out_shape=jax.ShapeDtypeStruct((rows, slots, LAGS, width), jnp.float32),
        scratch_shapes=[
            pltpu.VMEM((slots, nq, fq, kw, width), jnp.float32),
            pltpu.VMEM((slots, nq, fq, kw, width), jnp.float32),
            pltpu.VMEM((FREQS * 2 * rows, width), jnp.float32),
            pltpu.VMEM((2, OUT_ROWS, LAGS, width), jnp.float32),
            pltpu.SemaphoreType.DMA((slots, 2, nq)),
            pltpu.SemaphoreType.DMA((2,)),
        ],
        input_output_aliases=aliases,
        compiler_params=pltpu.CompilerParams(vmem_limit_bytes=VMEM_LIMIT),
        cost_estimate=pl.CostEstimate(
            flops=2 * slots * rows * LAGS * 2 * FREQS * width * 6, bytes_accessed=24 * 1024 * 1024, transcendentals=0
        ),
        name="correlate",
    )(*operands)


def plan_kernel(tiles, subs, slots, rounds, chunks, fq, rows, width, pair_ref, owner_ref, plan_ref):
    me, me_freq, me_sub = lax.axis_index("tile"), lax.axis_index("freq"), lax.axis_index("sub")
    freqs = lax.axis_size("freq")
    zero = jnp.int32(0)

    def bit(block):
        return jnp.left_shift(jnp.int32(1), block)

    def own(tile):
        return ((1 << subs) - 1) << (subs * tile)

    def up_to(tile):
        return (1 << (subs * (tile + 1))) - 1

    def pick(index, values):
        chosen = zero
        for key, value in values.items():
            chosen = jnp.where(index == key, value, chosen)
        return chosen

    def lowest(bits):
        return jnp.bitwise_and(bits, -bits)

    every = [[zero] * slots for _ in range(tiles)]
    rows_bit, cols_bit, filled = {}, {}, {}
    for k in range(slots):
        rows_bit[k], cols_bit[k], filled[k] = zero, zero, zero
        for t in range(tiles):
            pair = owner_ref[k, t]
            there = pair >= 0
            first = jnp.where(there, bit(pair_ref[0, jnp.maximum(pair, 0)]), 0)
            second = jnp.where(there, bit(pair_ref[1, jnp.maximum(pair, 0)]), 0)
            every[t][k] = first | second
            mine = me == t
            rows_bit[k] = jnp.where(mine, first, rows_bit[k])
            cols_bit[k] = jnp.where(mine, second, cols_bit[k])
            filled[k] = jnp.where(mine, there.astype(jnp.int32), filled[k])
    need = [functools.reduce(jnp.bitwise_or, every[t]) for t in range(tiles)]
    left_to_do = {}
    for t in range(tiles - 1):
        left_to_do[(1, t)] = functools.reduce(jnp.bitwise_or, need[t + 1 :]) & up_to(t)
        left_to_do[(-1, t + 1)] = functools.reduce(jnp.bitwise_or, need[: t + 1]) & ~up_to(t)
    todo = list(need)
    have = [jnp.int32(own(t)) for t in range(tiles)]
    places = [(bit(subs * me + me_sub), 0), (bit(subs * me + 1 - me_sub), 1)]

    def place(block_bit):
        where = jnp.int32(-1)
        for held_bit, index in places:
            where = jnp.where(jnp.logical_and(block_bit == held_bit, block_bit != 0), index, where)
        return where

    needed_rounds = jnp.int32(1)
    my_order = []
    for r in range(rounds):
        sel, over_freq = {}, {}
        for (step, t), want in left_to_do.items():
            cand = have[t] & want
            chosen = zero
            for u in range(tiles - 1, t, -1) if step > 0 else range(0, t):
                chosen = jnp.where(chosen == 0, lowest(cand & need[u]), chosen)
            sel[(step, t)] = chosen
        for t in range(tiles):
            ready = have[t] & todo[t]
            early = ready & every[t][0]
            over_freq[t] = jnp.where(early != 0, lowest(early), lowest(ready))
        for key in sel:
            left_to_do[key] = left_to_do[key] & ~sel[key]
        for t in range(tiles):
            todo[t] = todo[t] & ~over_freq[t]
            for step in (1, -1):
                if (step, t - step) in sel:
                    have[t] = have[t] | sel[(step, t - step)]
        plan_ref[3 * r] = place(pick(me, {t: sel[(1, t)] for t in range(tiles - 1)}))
        plan_ref[3 * r + 1] = place(pick(me, {t: sel[(-1, t)] for t in range(1, tiles)}))
        mine = pick(me, over_freq)
        plan_ref[3 * r + 2] = place(mine)
        my_order.append(mine)
        places.append((pick(me, {t + 1: sel[(1, t)] for t in range(tiles - 1)}), 2 + 2 * r))
        places.append((pick(me, {t - 1: sel[(-1, t)] for t in range(1, tiles)}), 3 + 2 * r))
        rest = functools.reduce(jnp.bitwise_or, todo)
        needed_rounds = needed_rounds + (rest != 0).astype(jnp.int32)
    plan_ref[3 * rounds] = needed_rounds
    base = 3 * rounds + 1
    plan_ref[base] = lax.rem(width - (me_sub * freqs + me_freq) * rows, width)
    n = 0
    for f, s in ((0, 0), (1, 0), (0, 1), (1, 1)):
        share = (me_freq ^ f) * subs + (me_sub ^ s)
        for c in range(chunks):
            plan_ref[base + 1 + n] = share * fq + c * (fq // chunks)
            n += 1
    for k in range(slots):
        for which, wanted in ((0, rows_bit[k]), (1, cols_bit[k])):
            at = zero
            for r in range(rounds):
                at = jnp.where(my_order[r] == wanted, r, at)
            plan_ref[base + 1 + n + 3 * k + which] = at
        plan_ref[base + 1 + n + 3 * k + 2] = filled[k]


def make_plan(pair_list, owner_slots, rounds, chunks, fq, rows, width):
    tiles, slots = owner_slots.shape
    smem = pl.BlockSpec(memory_space=pltpu.SMEM)
    return pl.pallas_call(
        functools.partial(plan_kernel, tiles, lax.axis_size("sub"), slots, rounds, chunks, fq, rows, width),
        in_specs=[smem, smem],
        out_specs=smem,
        out_shape=jax.ShapeDtypeStruct((3 * rounds + 2 + 4 * chunks + 3 * slots,), jnp.int32),
        name="make_plan",
    )(pair_list.T, owner_slots.T)


def choose_kernel(which, chunk, spans, unread, plan, *refs):
    count = len(which)
    held, outs = refs[: len(spans)], refs[len(spans) + unread : len(spans) + unread + count]
    stage, in_sems, out_sems = refs[len(spans) + unread + count :]
    depth = stage.shape[1]

    def load(i, n):
        src = held[n].at[pl.ds(chunk * depth, depth)] if spans[n] else held[n]
        return pltpu.make_async_copy(src, stage.at[i], in_sems.at[i])

    def store(i):
        return pltpu.make_async_copy(stage.at[i], outs[i], out_sems.at[i])

    for i, entry in enumerate(which):
        for n in range(len(spans)):

            @pl.when(plan[entry] == n)
            def _():
                load(i, n).start()

    for i, entry in enumerate(which):

        @pl.when(plan[entry] >= 0)
        def _():
            load(i, 0).wait()
            store(i).start()

    for i, entry in enumerate(which):

        @pl.when(plan[entry] >= 0)
        def _():
            store(i).wait()


def choose(plan, which, held, after, chunk, depth):
    spans = [a.shape[0] != depth for a in held]
    any_spec = pl.BlockSpec(memory_space=pl.ANY)
    out = jax.ShapeDtypeStruct((depth,) + held[0].shape[1:], jnp.float32)
    return pl.pallas_call(
        functools.partial(choose_kernel, which, chunk, spans, len(after)),
        in_specs=[pl.BlockSpec(memory_space=pltpu.SMEM)] + [any_spec] * (len(held) + len(after)),
        out_specs=[any_spec] * len(which),
        out_shape=[out] * len(which),
        scratch_shapes=[
            pltpu.VMEM((len(which),) + out.shape, jnp.float32),
            pltpu.SemaphoreType.DMA((len(which),)),
            pltpu.SemaphoreType.DMA((len(which),)),
        ],
        compiler_params=pltpu.CompilerParams(vmem_limit_bytes=VMEM_LIMIT),
        cost_estimate=pl.CostEstimate(flops=0, bytes_accessed=len(which) * 2 * depth * 32 * 512, transcendentals=0),
        name="choose",
    )(plan, *held, *after)


def relay_kernel(count, *refs):
    srcs, outs = refs[:count], refs[-count - 3 : -3]
    stage, in_sems, out_sems = refs[-3:]
    loads = [pltpu.make_async_copy(srcs[i], stage.at[i], in_sems.at[i]) for i in range(count)]
    stores = [pltpu.make_async_copy(stage.at[i], outs[i], out_sems.at[i]) for i in range(count)]
    for load in loads:
        load.start()
    for load, store in zip(loads, stores):
        load.wait()
        store.start()
    for store in stores:
        store.wait()


def relay(arrays, after):
    count = len(arrays)
    any_spec = pl.BlockSpec(memory_space=pl.ANY)
    return pl.pallas_call(
        functools.partial(relay_kernel, count),
        in_specs=[any_spec] * (count + 1),
        out_specs=[any_spec] * count,
        out_shape=[jax.ShapeDtypeStruct(a.shape, a.dtype) for a in arrays],
        scratch_shapes=[
            pltpu.VMEM((count,) + arrays[0].shape, jnp.float32),
            pltpu.SemaphoreType.DMA((count,)),
            pltpu.SemaphoreType.DMA((count,)),
        ],
        compiler_params=pltpu.CompilerParams(vmem_limit_bytes=VMEM_LIMIT),
        cost_estimate=pl.CostEstimate(flops=0, bytes_accessed=count * 2**20, transcendentals=0),
        name="relay",
    )(*arrays, after)


FEWEST, ROUNDS = 3, 5
CHUNKS = 2


def gather_all(slots, rows, windows, mine, passed, pair_list, owner_slots):
    freq_parts, subs = lax.axis_size("freq"), lax.axis_size("sub")
    me_tile, me_freq, me_sub = lax.axis_index("tile"), lax.axis_index("freq"), lax.axis_index("sub")
    fq, _, width = mine.shape
    nq = freq_parts * subs
    my_pairs = lax.dynamic_index_in_dim(owner_slots, me_tile, 0, keepdims=False)
    filled = (my_pairs >= 0).astype(jnp.int32)
    wanted = jnp.take(pair_list, jnp.maximum(my_pairs, 0), axis=0)
    shift = (width - (me_sub * freq_parts + me_freq) * rows) % width
    held = lax.all_gather(jnp.stack([mine, passed]), "tile")
    items = []
    for slot in range(slots):
        for which in range(2):
            block = wanted[slot, which]
            chosen = held[block // 2, (block % 2) ^ me_sub]
            items.append(lax.all_gather(chosen, ("freq", "sub")))
    srcs = [[item[q] for item in items] for q in range(nq)]
    first = jnp.arange(nq, dtype=jnp.int32) * fq
    meta = jnp.concatenate(
        [shift.reshape(1), first]
        + [jnp.stack([jnp.int32(2 * k), jnp.int32(2 * k + 1), filled[k]]) for k in range(slots)]
    ).astype(jnp.int32)
    return correlate(meta, 0, srcs, rows, slots, windows)


def in_rounds(count, slots, rows, windows, mine, passed, plan):
    tiles = lax.axis_size("tile")
    right = [(t, t + 1) for t in range(tiles - 1)]
    left = [(t + 1, t) for t in range(tiles - 1)]
    swap = [(0, 1), (1, 0)]
    depth = mine.shape[0] // CHUNKS
    held = [[mine, passed] for _ in range(CHUNKS)]
    srcs = [[] for _ in range(4 * CHUNKS)]
    for r in range(count):
        for c in range(CHUNKS):
            after = [srcs[n * CHUNKS + c][r - age] for n, age in ((1, 1), (2, 1), (3, 2)) if r >= age]
            last = r == count - 1
            chosen = choose(plan, [3 * r + 2] + [3 * r, 3 * r + 1] * (not last), held[c], after, c, depth)
            to_freq = chosen[0]
            crossed = lax.ppermute(to_freq, "freq", swap)
            if not last:
                held[c] = held[c] + [lax.ppermute(chosen[1], "tile", right), lax.ppermute(chosen[2], "tile", left)]
            srcs[c].append(to_freq)
            srcs[CHUNKS + c].append(crossed)
            srcs[2 * CHUNKS + c].append(lax.ppermute(to_freq, "sub", swap))
            if r < count - 1:
                srcs[3 * CHUNKS + c].append(lax.ppermute(crossed, "sub", swap))
    base = 3 * ROUNDS + 1
    before = [share[: count - 1] for share in srcs]
    sent = [share[-1] for share in srcs[:CHUNKS]]
    first = correlate(plan, base, before, rows, slots, windows, count - 1, False, sent)
    for c, copied in enumerate(relay([share[-1] for share in srcs[CHUNKS : 2 * CHUNKS]], first)):
        srcs[3 * CHUNKS + c].append(lax.ppermute(copied, "sub", swap))
    return correlate(plan, base, srcs, rows, slots, windows, count - 1, True, (), first)


def body(spectra, pair_list, owner_slots):
    tiles, freq_parts, subs = lax.axis_size("tile"), lax.axis_size("freq"), lax.axis_size("sub")
    _, windows, band, width = spectra.shape
    slots = owner_slots.shape[1]
    fq = band // subs
    rows = width // (freq_parts * subs)
    me_sub = lax.axis_index("sub")
    other = whiten(spectra, 1 - me_sub, fq)
    passed = lax.ppermute(other, "sub", [(0, 1), (1, 0)])
    mine = whiten(spectra, me_sub, fq)
    whole = functools.partial(gather_all, slots, rows, windows)
    if freq_parts != 2 or tiles > 4:
        return whole(mine, passed, pair_list, owner_slots)
    plan = make_plan(pair_list, owner_slots, ROUNDS, CHUNKS, fq, rows, width)
    branches = [
        functools.partial(lambda n, a, b, p, pairs, owners: in_rounds(n, slots, rows, windows, a, b, p), n)
        for n in range(FEWEST, ROUNDS + 1)
    ]
    branches.append(lambda a, b, p, pairs, owners: whole(a, b, pairs, owners))
    return lax.switch(
        jnp.maximum(plan[3 * ROUNDS], FEWEST) - FEWEST, branches, mine, passed, plan, pair_list, owner_slots
    )


def solution(mesh):
    in_specs = (P("day", None, "freq", ("tile", "sub")), P(), P())
    out_specs = P(("sub", "freq"), ("day", "tile"), None, None)
    return jax.shard_map(body, mesh=mesh, in_specs=in_specs, out_specs=out_specs, check_vma=False)
```
